256 devices in a mesh: dp: 32 (over x, z), fsdp: 8 (over y, core).
Axes of the slice: x: 4, y: 4, z: 8, core: 2. Of those that a mesh axis runs over, the one named last changes fastest.
Arguments:
- inputs: bfloat16 [24576, 1152], P('dp'), may hold values from -6 to 6
- cotangent: bfloat16 [24576, 1152], P('dp')
- gate_weight: bfloat16 [1152, 6912], P(None, 'fsdp'), may hold values from -0.1875 to 0.1875
- up_weight: bfloat16 [1152, 6912], P(None, 'fsdp')
- down_weight: bfloat16 [6912, 1152], P('fsdp'), may hold values from -0.078125 to 0.078125
- live_counts: int32 [32], P('dp'), may hold values from 1 to 3, as said below
- noise_gate: float32 [1152, 6912], P('dp', 'fsdp'), may hold values from -6 to 6
- noise_up: float32 [1152, 6912], P('dp', 'fsdp'), may hold values from -6 to 6
- noise_down: float32 [6912, 1152], P('fsdp', 'dp'), may hold values from -6 to 6
Outputs:
- grad_gate: float32 [1152, 6912], P('dp', 'fsdp')
- grad_up: float32 [1152, 6912], P('dp', 'fsdp')
- grad_down: float32 [6912, 1152], P('fsdp', 'dp')
The draws below stay inside these ranges and needn't reach their ends.
Inputs may be any that keep to these rules, and one draw needn't show every extreme that they name: The first live_counts[d] slots of data-parallel index d hold its sampled sequences; the others are unused.
All inputs are finite; a program needn't handle non-finite values.
Results may differ from the reference program's by a relative error of at most 0.0038.
Values may be sent and summed in bfloat16 or wider, within the bound.
A program may use at most 128 MiB of HBM per device.

```python
import math
import jax
import jax.numpy as jnp
from jax import lax

D = 1152
FF = 6912
SEQ = 256
SLOTS = 3
ROWS = 24576
N_DP = 32


def draw_cotangent(key, part):
    key = jax.random.fold_in(key, 12)
    scale_key, value_key = jax.random.split(key, 2)
    scales = 10.0 ** jax.random.uniform(scale_key, (N_DP * SLOTS, 1, 1), jnp.float32, -2.0, 0.0)
    values = jax.random.normal(value_key, (N_DP * SLOTS, SEQ, D), jnp.float32)
    return (values * scales).reshape(N_DP * SLOTS * SEQ, D).astype(jnp.bfloat16)


def draw_up_weight(key, part):
    key = jax.random.fold_in(key, 13)
    value_key, factor_key = jax.random.split(key)
    ramp_up = 0.55 * 3.0 ** (jnp.arange(FF, dtype=jnp.float32) / FF)
    spread = jnp.exp(jax.random.uniform(factor_key, (FF,), jnp.float32, -0.35, 0.35))
    values = jax.random.normal(value_key, (D, FF), jnp.float32)
    return (values * (ramp_up * spread)[None, :] / jnp.sqrt(jnp.float32(D))).astype(jnp.bfloat16)


def draw_live_counts(key, part):
    key = jax.random.fold_in(key, 11)
    toss_key, shuffle_key = jax.random.split(key)
    tosses = jax.random.randint(toss_key, (N_DP, SLOTS - 1), 0, 2)
    counts = 1 + jnp.sum(tosses, axis=1).astype(jnp.int32)
    shuffled = jax.random.permutation(shuffle_key, N_DP)
    counts = counts.at[shuffled[0]].set(SLOTS)
    counts = counts.at[shuffled[1]].set(1)
    return counts.astype(jnp.int32)


def levels(own_key, extent, cuts, least, top_value):
    level = 1.0
    for axis_at, blocks in cuts:
        heights = jax.random.uniform(jax.random.fold_in(jax.random.fold_in(own_key, 6), axis_at), (blocks,), jnp.float32, least / len(cuts), top_value / len(cuts))
        level = level * jnp.repeat(jnp.exp(heights), extent[axis_at] // blocks).reshape((-1,) + (1,) * (len(extent) - 1 - axis_at))
    return level


def noise(rng, extent, scale, limit, pieces=(), kind=jnp.bfloat16):
    level = levels(rng, extent, pieces, -0.22, 0.18) if pieces else 1.0
    values = jax.random.normal(rng, extent, jnp.float32) * scale * level
    return jnp.minimum(jnp.maximum(values, -limit), limit).astype(kind)


def setup_inputs(seed: int = 0) -> dict:
    keys = jax.random.split(jax.random.key(seed), 10)
    return {
        "inputs": noise(keys[0], (ROWS, D), 1.0, 6.0, ((0, 32),)),
        "cotangent": draw_cotangent(jax.random.fold_in(keys[9], 71), 0),
        "gate_weight": noise(keys[2], (D, FF), D ** -0.5, 0.1875, ((1, 8),)),
        "up_weight": draw_up_weight(jax.random.fold_in(keys[9], 71), 0),
        "down_weight": noise(keys[4], (FF, D), FF ** -0.5, 0.078125, ((0, 8),)),
        "live_counts": draw_live_counts(jax.random.fold_in(keys[9], 71), 0),
        "noise_gate": noise(keys[6], (D, FF), 1.0, 6.0, ((0, 32), (1, 8)), jnp.float32),
        "noise_up": noise(keys[7], (D, FF), 1.0, 6.0, ((0, 32), (1, 8)), jnp.float32),
        "noise_down": noise(keys[8], (FF, D), 1.0, 6.0, ((0, 8), (1, 32)), jnp.float32),
    }


gelu_scale = 0.7978845608028654
gelu_cube = 0.044715

def gelu_pair(values):
    tanh_arg = gelu_scale * (values + gelu_cube * values * values * values)
    tangent = jnp.tanh(tanh_arg)
    gelu_value = 0.5 * values * (1.0 + tangent)
    gelu_slope = 0.5 * (1.0 + tangent) + 0.5 * values * (1.0 - tangent * tangent) * gelu_scale * (1.0 + 3.0 * gelu_cube * values * values)
    return (gelu_value, gelu_slope)

def reference(inputs, cotangent, gate_weight, up_weight, down_weight, live_counts, noise_gate, noise_up, noise_down):
    bound = 0.1 * math.sqrt(SEQ * D * FF)
    seq_rows = inputs.reshape(N_DP * SLOTS, SEQ, D)
    seq_grad = cotangent.reshape(N_DP * SLOTS, SEQ, D)
    live_mask = (jnp.arange(SLOTS, dtype=jnp.int32)[None, :] < live_counts[:, None]).reshape(-1).astype(jnp.float32)

    def per_example(state_in, example):
        rows_now, grad_now, is_live = example
        gate_pre = jnp.dot(rows_now, gate_weight, preferred_element_type=jnp.float32)
        up_pre = jnp.dot(rows_now, up_weight, preferred_element_type=jnp.float32)
        gelu_value, gelu_slope = gelu_pair(gate_pre)
        hidden = (gelu_value * up_pre).astype(jnp.bfloat16)
        back_grad = jnp.dot(grad_now, down_weight.T, preferred_element_type=jnp.float32)
        d_gate = (back_grad * up_pre * gelu_slope).astype(jnp.bfloat16)
        d_up = (back_grad * gelu_value).astype(jnp.bfloat16)
        gram_rows = jnp.dot(rows_now, rows_now.T, preferred_element_type=jnp.float32)
        gram_mix = jnp.dot(d_gate, d_gate.T, preferred_element_type=jnp.float32) + jnp.dot(d_up, d_up.T, preferred_element_type=jnp.float32)
        gram_hidden = jnp.dot(hidden, hidden.T, preferred_element_type=jnp.float32)
        gram_out = jnp.dot(grad_now, grad_now.T, preferred_element_type=jnp.float32)
        squared = jnp.sum(gram_rows * gram_mix) + jnp.sum(gram_hidden * gram_out)
        grad_norm = jnp.sqrt(jnp.maximum(squared, 0.0))
        factor = is_live * bound / jnp.maximum(grad_norm, bound)
        scaled_gate = (d_gate.astype(jnp.float32) * factor).astype(jnp.bfloat16)
        scaled_up = (d_up.astype(jnp.float32) * factor).astype(jnp.bfloat16)
        scaled_out = (grad_now.astype(jnp.float32) * factor).astype(jnp.bfloat16)
        sum_gate, sum_up, sum_down = state_in
        sum_gate = sum_gate + jnp.dot(rows_now.T, scaled_gate, preferred_element_type=jnp.float32)
        sum_up = sum_up + jnp.dot(rows_now.T, scaled_up, preferred_element_type=jnp.float32)
        sum_down = sum_down + jnp.dot(hidden.T, scaled_out, preferred_element_type=jnp.float32)
        return ((sum_gate, sum_up, sum_down), None)
    start_state = (jnp.zeros((D, FF), jnp.float32), jnp.zeros((D, FF), jnp.float32), jnp.zeros((FF, D), jnp.float32))
    final_state, _ = lax.scan(per_example, start_state, (seq_rows, seq_grad, live_mask))
    return (final_state[0] + noise_gate, final_state[1] + noise_up, final_state[2] + noise_down)
```

```python
import functools
import math

import jax
import jax.numpy as jnp
from jax import lax
from jax.experimental import pallas as pl
from jax.experimental.pallas import tpu as pltpu
from jax.sharding import PartitionSpec as P

D = 1152
FF = 6912
SEQ = 256
SLOTS = 3
NX = 4
NZ = 8
OWN = D // (NX * NZ)
XROWS = D // NX
ZROWS = D // NZ
LANE = 128
F32 = jnp.float32
BF16 = jnp.bfloat16
MESH = pl.DeviceIdType.MESH

gelu_scale = 0.7978845608028654
gelu_cube = 0.044715

HP = 896
UP_A = 512
WA = HP + UP_A
WU_B = HP - UP_A
WB = WU_B + HP
A_HALF = ((0, 768), (768, 1408))
B_HALF = ((0, 640), (640, 1280))
A2_TILES = (5, 6)
B2_TILES = (5, 5)


def pad16(n):
    return (n + 15) // 16 * 16


A2_ROWS = tuple(pad16(OWN * t) for t in A2_TILES)
B2_ROWS = tuple(pad16(OWN * t) for t in B2_TILES)


def gelu_pair(values):
    square = values * values
    tangent = jnp.tanh(values * (gelu_scale + (gelu_scale * gelu_cube) * square))
    half_sum = 0.5 + 0.5 * tangent
    gelu_value = values * half_sum
    gelu_slope = half_sum + (0.5 * values) * (1.0 - tangent * tangent) * (
        gelu_scale + (3.0 * gelu_scale * gelu_cube) * square
    )
    return gelu_value, gelu_slope


def nt(a, b):
    return lax.dot_general(a, b, (((1,), (1,)), ((), ())), preferred_element_type=F32)


def nn(a, b):
    return lax.dot_general(a, b, (((1,), (0,)), ((), ())), preferred_element_type=F32)


def kernel(
    n_f, seq, hidden, bound,
    live_ref, x_hbm, c_hbm, wg_hbm, wu_hbm, wd_hbm,
    gate_ref, up_ref, down_ref,
    xv, cv, wgv, wuv, wdv,
    hid, dg, du, mix_a, mix_b,
    stage, perm, xt, xt_b, ct_b,
    nrm_send, nrm_recv,
    xs, xr, zs, zr, sum_a, sum_b,
    a2_0, a2_1, as_0, ar_0, as_1, ar_1,
    b2, bs, br,
    load_sem, nrm_ssem, nrm_rsem, x_ssem, x_rsem, z_ssem, z_rsem, a_ssem, a_rsem, b_ssem, b_rsem,
):
    rows = SLOTS * seq
    dp = lax.axis_index("dp")
    fs = lax.axis_index("fsdp")
    mx = dp // NZ
    mz = dp % NZ

    def at_x(k):
        return (mx + (k + NX)) % NX

    def at_z(k):
        return (mz + (k + NZ)) % NZ

    def x_dev(k):
        return (at_x(k) * NZ + mz, fs)

    def z_dev(k):
        return (mx * NZ + at_z(k), fs)

    def f_dev(k):
        return (dp, (fs + k) % n_f)

    loads = [
        pltpu.make_async_copy(src, dst, load_sem.at[i])
        for i, (src, dst) in enumerate(
            ((x_hbm, xv), (wg_hbm, wgv), (wu_hbm, wuv), (c_hbm, cv), (wd_hbm, wdv))
        )
    ]
    for load in loads:
        load.start()

    barrier = pltpu.get_barrier_semaphore()
    peers = [x_dev(1), x_dev(-1), z_dev(1), z_dev(-1)] + [f_dev(k) for k in range(1, n_f)]
    for peer in peers:
        pl.semaphore_signal(barrier, inc=1, device_id=peer, device_id_type=MESH)

    for buf in (hid, dg, du):
        buf[:, HP - LANE : HP] = jnp.zeros((rows, LANE), BF16)
    for buf in (a2_0, a2_1, b2):
        buf[...] = jnp.zeros_like(buf)
    for load in loads:
        load.wait()

    edges = list(range(0, hidden, 256)) + [hidden]

    def slot_terms(e, carry):
        r = pl.ds(pl.multiple_of(e * seq, seq), seq)
        xe = xv[r, :]
        ce = cv[r, :]
        for lo, hi in zip(edges[:-1], edges[1:]):
            gate_pre = nn(xe, wgv[:, lo:hi])
            up_pre = nn(xe, wuv[:, lo:hi])
            back = nt(ce, wdv[lo:hi, :])
            gelu_value, gelu_slope = gelu_pair(gate_pre)
            hid[r, lo:hi] = (gelu_value * up_pre).astype(BF16)
            dg[r, lo:hi] = (back * up_pre * gelu_slope).astype(BF16)
            du[r, lo:hi] = (back * gelu_value).astype(BF16)
        dge, due, he = dg[r, :], du[r, :], hid[r, :]
        terms = nt(xe, xe) * (nt(dge, dge) + nt(due, due)) + nt(he, he) * nt(ce, ce)
        part = terms[:, 0:LANE]
        for lo in range(LANE, seq, LANE):
            part = part + terms[:, lo : lo + LANE]
        nrm_send[pl.ds(pl.multiple_of(e * 8, 8), 8), :] = part.reshape(seq // 8, 8, LANE).sum(axis=0)
        return carry

    lax.fori_loop(0, SLOTS, slot_terms, 0)

    pl.semaphore_wait(barrier, len(peers))

    def remote(src, dst, ssem, rsem, dev):
        copy = pltpu.make_async_remote_copy(
            src_ref=src, dst_ref=dst, send_sem=ssem, recv_sem=rsem, device_id=dev, device_id_type=MESH
        )
        copy.start()
        return copy

    sends = []
    norm_copies = [
        remote(nrm_send, nrm_recv.at[k - 1], nrm_ssem.at[k - 1], nrm_rsem.at[k - 1], f_dev(k))
        for k in range(1, n_f)
    ]

    def reorder(dst):
        for ox in range(NX):
            for oz in range(NZ):
                src_at = OWN * (NZ * ox + oz)
                dst_at = OWN * (NX * oz + ox)
                dst[dst_at : dst_at + OWN, :] = stage[src_at : src_at + OWN, :]

    turned = xv[...].T
    xt[...] = turned
    stage[...] = turned.astype(F32)
    reorder(perm)
    xt_b[...] = perm[...].astype(BF16)
    stage[...] = cv[...].T.astype(F32)
    reorder(perm)

    for copy in norm_copies:
        copy.wait_recv()
    total = nrm_send[...]
    for k in range(n_f - 1):
        total = total + nrm_recv[k]
    live = live_ref[0]
    for e in range(SLOTS):
        squared = jnp.sum(total[8 * e : 8 * e + 8, :], axis=(0, 1), keepdims=True)
        is_live = jnp.where(e < live, 1.0, 0.0).astype(F32)
        factor = is_live * bound / jnp.maximum(jnp.sqrt(jnp.maximum(squared, 0.0)), bound)
        lo, hi = e * seq, (e + 1) * seq
        ct_b[:, lo:hi] = (perm[:, lo:hi] * factor).astype(BF16)
        mix_b[lo:hi, :] = (du[lo:hi, UP_A:HP].astype(F32) * factor).astype(BF16)
        mix_a[lo:hi, 0:HP] = (dg[lo:hi, :].astype(F32) * factor).astype(BF16)
        mix_a[lo:hi, HP:WA] = (du[lo:hi, 0:UP_A].astype(F32) * factor).astype(BF16)

    def prod_a(chunk, h):
        lo, hi = A_HALF[h]
        r = pl.ds(pl.multiple_of(chunk * XROWS, XROWS), XROWS)
        return nn(xt[r, :], mix_a[:, lo:hi])

    def prod_b(chunk, h):
        lo, hi = B_HALF[h]
        r = pl.ds(pl.multiple_of(chunk * ZROWS, ZROWS), ZROWS)
        if h == 0:
            return jnp.concatenate(
                [nn(xt_b[r, :], mix_b[...]), nn(ct_b[r, :], hid[:, 0 : hi - WU_B])], axis=1
            )
        return nn(ct_b[r, :], hid[:, lo - WU_B : hi - WU_B])

    x_copy = {}

    def x_width(way, step):
        h = (way + step) % 2
        return A_HALF[h][1] - A_HALF[h][0]

    def send_x(step):
        for way in range(2):
            sign = 1 - 2 * way
            h = (way + step) % 2
            dist = 2 if step == 0 else 1
            value = prod_a(at_x(sign * dist), h)
            i = 3 * way + step
            w = x_width(way, step)
            if step == 2:
                x_copy[3 * way].wait_recv()
                value = value + xr[3 * way, :, 0:w].astype(F32)
            xs[i, :, 0:w] = value.astype(BF16)
            x_copy[i] = remote(
                xs.at[i, :, pl.ds(0, w)], xr.at[i, :, pl.ds(0, w)], x_ssem.at[i], x_rsem.at[i], x_dev(sign)
            )

    z_copy = {}

    def send_z(step):
        for way in range(2):
            sign = 1 - 2 * way
            h = (way + step) % 2
            dist = 4 - (step + 1) // 2
            value = prod_b(at_z(sign * dist), h)
            i = 7 * way + step
            if step >= 2:
                z_copy[i - 2].wait_recv()
                value = value + zr[i - 2].astype(F32)
            zs[i] = value.astype(BF16)
            z_copy[i] = remote(zs.at[i], zr.at[i], z_ssem.at[i], z_rsem.at[i], z_dev(sign))

    send_z(0)
    send_x(0)
    send_z(1)
    send_x(1)
    send_z(2)
    send_z(3)
    send_x(2)
    send_z(4)
    send_z(5)
    send_z(6)

    for h in range(2):
        lo, hi = A_HALF[h]
        value = prod_a(mx, h)
        for way in range(2):
            step = 2 if (way + 2) % 2 == h else 1
            i = 3 * way + step
            x_copy[i].wait_recv()
            value = value + xr[i, :, 0 : hi - lo].astype(F32)
        sum_a[:, lo:hi] = value
    a2 = (a2_0, a2_1)
    for oz in range(NZ):
        col = 0
        for h in range(2):
            for t in range(A2_TILES[h]):
                at = oz * A2_ROWS[h] + OWN * t
                a2[h][at : at + OWN, :] = sum_a[OWN * oz : OWN * oz + OWN, col : col + LANE]
                col += LANE

    a_bufs = ((as_0, ar_0), (as_1, ar_1))
    a_copy = {}
    a_slot = {}

    def send_a(step):
        for way in range(2):
            sign = 1 - 2 * way
            h = (way + step) % 2
            dist = 4 - (step + 1) // 2
            n = A2_ROWS[h]
            value = a2[h][pl.ds(pl.multiple_of(at_z(sign * dist) * n, n), n), :]
            i = 7 * way + step
            sbuf, rbuf = a_bufs[h]
            slot = 4 * way + step // 2
            if step >= 2:
                a_copy[i - 2].wait_recv()
                value = value + rbuf[4 * way + (step - 2) // 2].astype(F32)
            sbuf[slot] = value.astype(BF16)
            a_copy[i] = remote(sbuf.at[slot], rbuf.at[slot], a_ssem.at[i], a_rsem.at[i], z_dev(sign))

    send_a(0)
    send_a(1)

    for h in range(2):
        lo, hi = B_HALF[h]
        value = prod_b(mz, h)
        for way in range(2):
            step = 6 if (way + 6) % 2 == h else 5
            i = 7 * way + step
            z_copy[i].wait_recv()
            value = value + zr[i].astype(F32)
        sum_b[:, lo:hi] = value
    for ox in range(NX):
        col = 0
        for h in range(2):
            for t in range(B2_TILES[h]):
                at = ox * B2_ROWS[h] + OWN * t
                b2[h, at : at + OWN, :] = sum_b[OWN * ox : OWN * ox + OWN, col : col + LANE]
                col += LANE

    b_copy = {}

    def send_b(step):
        for way in range(2):
            sign = 1 - 2 * way
            h = (way + step) % 2
            dist = 2 if step == 0 else 1
            n = B2_ROWS[h]
            value = b2[h, pl.ds(pl.multiple_of(at_x(sign * dist) * n, n), n), :]
            i = 3 * way + step
            if step == 2:
                b_copy[3 * way].wait_recv()
                value = value + br[3 * way].astype(F32)
            bs[i] = value.astype(BF16)
            b_copy[i] = remote(bs.at[i], br.at[i], b_ssem.at[i], b_rsem.at[i], x_dev(sign))

    send_b(0)
    send_b(1)
    send_a(2)
    send_a(3)
    send_b(2)
    send_a(4)
    send_a(5)
    send_a(6)

    def put(col, block):
        start, width = col, LANE
        if start < HP:
            ref, at = gate_ref, start
        elif start < 2 * HP:
            ref, at = up_ref, start - HP
        else:
            ref, at = down_ref, start - 2 * HP
        width = min(LANE, hidden - at)
        ref[:, at : at + width] = block[:, 0:width]

    col = WA
    for h in range(2):
        n = B2_ROWS[h]
        value = b2[h, pl.ds(pl.multiple_of(mx * n, n), n), :]
        for way in range(2):
            step = 2 if (way + 2) % 2 == h else 1
            i = 3 * way + step
            b_copy[i].wait_recv()
            value = value + br[i].astype(F32)
        b2[h, 0:n, :] = value
        for t in range(B2_TILES[h]):
            put(col, b2[h, OWN * t : OWN * t + OWN, :])
            col += LANE
    col = 0
    for h in range(2):
        n = A2_ROWS[h]
        value = a2[h][pl.ds(pl.multiple_of(mz * n, n), n), :]
        for way in range(2):
            step = 6 if (way + 6) % 2 == h else 5
            i = 7 * way + step
            a_copy[i].wait_recv()
            value = value + a_bufs[h][1][4 * way + step // 2].astype(F32)
        a2[h][0:n, :] = value
        for t in range(A2_TILES[h]):
            put(col, a2[h][OWN * t : OWN * t + OWN, :])
            col += LANE

    for copies in (norm_copies, x_copy.values(), z_copy.values(), a_copy.values(), b_copy.values()):
        for copy in copies:
            copy.wait_send()


def per_device(
    n_f, inputs, cotangent, gate_weight, up_weight, down_weight, live_counts, noise_gate, noise_up, noise_down
):
    rows = inputs.shape[0]
    seq = rows // SLOTS
    hidden = gate_weight.shape[1]
    bound = 0.1 * math.sqrt(SEQ * D * FF)
    any_spec = pl.BlockSpec(memory_space=pl.ANY)
    vmem = pl.BlockSpec(memory_space=pltpu.VMEM)
    dma = pltpu.SemaphoreType.DMA
    out = jax.ShapeDtypeStruct((OWN, hidden), F32)
    gate, up, down = pl.pallas_call(
        functools.partial(kernel, n_f, seq, hidden, bound),
        out_shape=(out, out, out),
        in_specs=[pl.BlockSpec(memory_space=pltpu.SMEM)] + [any_spec] * 5,
        out_specs=(vmem, vmem, vmem),
        scratch_shapes=[
            pltpu.VMEM((rows, D), BF16),
            pltpu.VMEM((rows, D), BF16),
            pltpu.VMEM((D, hidden), BF16),
            pltpu.VMEM((D, hidden), BF16),
            pltpu.VMEM((hidden, D), BF16),
            pltpu.VMEM((rows, HP), BF16),
            pltpu.VMEM((rows, HP), BF16),
            pltpu.VMEM((rows, HP), BF16),
            pltpu.VMEM((rows, WA), BF16),
            pltpu.VMEM((rows, WU_B), BF16),
            pltpu.VMEM((D, rows), F32),
            pltpu.VMEM((D, rows), F32),
            pltpu.VMEM((D, rows), BF16),
            pltpu.VMEM((D, rows), BF16),
            pltpu.VMEM((D, rows), BF16),
            pltpu.VMEM((8 * SLOTS, LANE), F32),
            pltpu.VMEM((max(n_f - 1, 1), 8 * SLOTS, LANE), F32),
            pltpu.VMEM((6, XROWS, 768), BF16),
            pltpu.VMEM((6, XROWS, 768), BF16),
            pltpu.VMEM((14, ZROWS, 640), BF16),
            pltpu.VMEM((14, ZROWS, 640), BF16),
            pltpu.VMEM((XROWS, WA), F32),
            pltpu.VMEM((ZROWS, WB), F32),
            pltpu.VMEM((NZ * A2_ROWS[0], LANE), F32),
            pltpu.VMEM((NZ * A2_ROWS[1], LANE), F32),
            pltpu.VMEM((8, A2_ROWS[0], LANE), BF16),
            pltpu.VMEM((8, A2_ROWS[0], LANE), BF16),
            pltpu.VMEM((8, A2_ROWS[1], LANE), BF16),
            pltpu.VMEM((8, A2_ROWS[1], LANE), BF16),
            pltpu.VMEM((2, NX * B2_ROWS[0], LANE), F32),
            pltpu.VMEM((6, B2_ROWS[0], LANE), BF16),
            pltpu.VMEM((6, B2_ROWS[0], LANE), BF16),
            dma((5,)),
            dma((max(n_f - 1, 1),)),
            dma((max(n_f - 1, 1),)),
            dma((6,)),
            dma((6,)),
            dma((14,)),
            dma((14,)),
            dma((14,)),
            dma((14,)),
            dma((6,)),
            dma((6,)),
        ],
        compiler_params=pltpu.CompilerParams(
            collective_id=0, has_side_effects=True, vmem_limit_bytes=60 * 1024 * 1024
        ),
    )(live_counts, inputs, cotangent, gate_weight, up_weight, down_weight)
    return gate + noise_gate, up + noise_up, down.T + noise_down


def solution(mesh):
    in_specs = (
        P("dp", None),
        P("dp", None),
        P(None, "fsdp"),
        P(None, "fsdp"),
        P("fsdp", None),
        P("dp"),
        P("dp", "fsdp"),
        P("dp", "fsdp"),
        P("fsdp", "dp"),
    )
    out_specs = (P("dp", "fsdp"), P("dp", "fsdp"), P("fsdp", "dp"))
    return jax.shard_map(
        functools.partial(per_device, mesh.shape["fsdp"]),
        mesh=mesh, in_specs=in_specs, out_specs=out_specs, check_vma=False,
    )
```

```python
import functools
import math

import jax
import jax.numpy as jnp
from jax import lax
from jax.experimental import pallas as pl
from jax.experimental.pallas import tpu as pltpu
from jax.sharding import PartitionSpec as P

D = 1152
FF = 6912
SEQ = 256
SLOTS = 3
NX = 4
NZ = 8
OWN = D // (NX * NZ)
XROWS = D // NX
ZROWS = D // NZ
LANE = 128
F32 = jnp.float32
BF16 = jnp.bfloat16
MESH = pl.DeviceIdType.MESH

gelu_scale = 0.7978845608028654
gelu_cube = 0.044715

HP = 896
GROUPS = (
    ("z", ((("up", 512, 896),), (("down", 0, 256),)), "direct"),
    ("x", ((("gate", 0, 512),), (("gate", 512, 896), ("up", 0, 128),)), "chain"),
    ("z", ((("down", 256, 512),), (("down", 512, 896),)), "direct"),
    ("x", ((("up", 128, 384),), (("up", 384, 512),)), "tree"),
)
ORDER = (
    (2, 1, 0), (1, 1, 0), (2, 1, 1), (0, 1, 0), (0, 1, 1), (1, 1, 1), (2, 1, 2), (2, 1, 3),
    (0, 1, 2), (1, 1, 2), (0, 1, 3), (2, 1, 4), (2, 1, 5), (3, 1, 0), (0, 1, 4), (3, 1, 1),
    (0, 1, 5), (1, 0, 0), (2, 1, 6), (1, 2, 0), (3, 1, 2), (1, 2, 1), (0, 1, 6), (2, 0, 0),
    (2, 2, 0), (1, 2, 2), (1, 2, 3), (3, 0, 0), (3, 2, 0), (3, 2, 1), (0, 0, 0), (0, 2, 0),
    (1, 2, 4), (1, 2, 5), (2, 3, 0), (3, 2, 2), (1, 2, 6), (0, 3, 0), (3, 3, 0), (1, 3, 0),
)
RING = {"x": NX, "z": NZ}


def pad16(n):
    return (n + 15) // 16 * 16


def gelu_pair(values):
    square = values * values
    tangent = jnp.tanh(values * (gelu_scale + (gelu_scale * gelu_cube) * square))
    half_sum = 0.5 + 0.5 * tangent
    gelu_value = values * half_sum
    gelu_slope = half_sum + (0.5 * values) * (1.0 - tangent * tangent) * (
        gelu_scale + (3.0 * gelu_scale * gelu_cube) * square
    )
    return gelu_value, gelu_slope


def nt(a, b):
    return lax.dot_general(a, b, (((1,), (1,)), ((), ())), preferred_element_type=F32)


def nn(a, b):
    return lax.dot_general(a, b, (((1,), (0,)), ((), ())), preferred_element_type=F32)


def width_of(half):
    return sum(hi - lo for _, lo, hi in half)


def chain(axis):
    last, far = (3, 2) if axis == "x" else (7, 4)
    sends = []
    for step in range(last):
        for way in range(2):
            sign = 1 - 2 * way
            halves = ((way + step) % 2,)
            owner = sign * (far - (step + 1) // 2)
            sends.append((step, way, halves, owner, sign, (len(sends) - 4,) if step >= 2 else ()))
    return sends


def direct(axis):
    far = RING[axis] // 2
    sends = []
    for dist in range(far, 0, -1):
        for way in range(2):
            at = dist * (1 - 2 * way)
            sends.append((0, way, (way,) if dist == far else (0, 1), at, at, ()))
    return sends


def tree(axis):
    sends = []
    for way in range(2):
        sign = 1 - 2 * way
        sends.append((0, way, (way,), 4 * sign, 2 * sign, ()))
    for way in range(2):
        sign = 1 - 2 * way
        sends.append((0, way, (0, 1), 3 * sign, sign, ()))
    for way in range(2):
        sign = 1 - 2 * way
        sends.append((1, way, (0, 1), sign, sign, ()))
    for way in range(2):
        sign = 1 - 2 * way
        sends.append((2, way, (0, 1), 2 * sign, 2 * sign, (way, 2 + way)))
    return sends


SECOND = {"chain": chain, "direct": direct, "tree": tree}


def packed_rows(g):
    return [pad16(OWN * width_of(half) // LANE) for half in GROUPS[g][1]]


def plan():
    sends = {}
    for g, (axis, _, mode) in enumerate(GROUPS):
        other = "z" if axis == "x" else "x"
        sends[g, 1] = (axis, chain(axis))
        sends[g, 2] = (other, SECOND[mode](other))
    return sends


def scratch_plan():
    shapes = {}
    for g, (axis, halves, _) in enumerate(GROUPS):
        rows = XROWS if axis == "x" else ZROWS
        other = NZ if axis == "x" else NX
        first = RING[axis] - 1
        for h, half in enumerate(halves):
            width = width_of(half)
            shapes[g, h, "s1"] = ((first, rows, width), BF16)
            shapes[g, h, "r1"] = ((first, rows, width), BF16)
            shapes[g, h, "sum"] = ((rows, width), F32)
        packed = packed_rows(g)
        shapes[g, "pack"] = ((other * sum(packed), LANE), F32)
        total = sum(packed[h] for send in plan()[g, 2][1] for h in send[2])
        shapes[g, "s2"] = ((total, LANE), BF16)
        shapes[g, "r2"] = ((total, LANE), BF16)
    return shapes


def total_sends():
    return sum(len(sends) for _, sends in plan().values())


def kernel(
    n_f, seq, hidden, bound,
    live_ref, x_hbm, c_hbm, wg_hbm, wu_hbm, wd_hbm,
    gate_ref, up_ref, down_ref,
    xv, cv, wgv, wuv, wrem, wdv,
    hid, dg, du,
    stage, perm, xt, xt_z, ct_z,
    nrm_send, nrm_recv,
    fin, load_sem, nrm_ssem, nrm_rsem, ssem, rsem,
    *group_refs,
):
    rows = SLOTS * seq
    dp = lax.axis_index("dp")
    fs = lax.axis_index("fsdp")
    mine = {"x": dp // NZ, "z": dp % NZ}
    buf = dict(zip(scratch_plan(), group_refs))

    def at(axis, k):
        return (mine[axis] + (k + RING[axis])) % RING[axis]

    def neighbour(axis, k):
        if axis == "x":
            return (at("x", k) * NZ + mine["z"], fs)
        return (mine["x"] * NZ + at("z", k), fs)

    def f_dev(k):
        return (dp, (fs + k) % n_f)

    full = hidden // 256 * 256
    rest = hidden - full
    pairs = [(x_hbm, xv)]
    for lo in range(0, full, 256):
        r = pl.ds(lo, 256)
        pairs += [(wg_hbm.at[r, :], wgv.at[r, :]), (wu_hbm.at[r, :], wuv.at[r, :])]
        if lo == 0:
            pairs.append((c_hbm, cv))
        pairs.append((wd_hbm.at[r, :], wdv.at[r, :]))
    r = pl.ds(full, rest)
    pairs.append((wg_hbm.at[r, :], wrem.at[pl.ds(0, rest), :]))
    pairs.append((wu_hbm.at[r, :], wrem.at[pl.ds(LANE, rest), :]))
    pairs.append((wd_hbm.at[r, :], wdv.at[r, :]))
    loads = [pltpu.make_async_copy(src, dst, load_sem.at[i]) for i, (src, dst) in enumerate(pairs)]
    for load in loads:
        load.start()

    barrier = pltpu.get_barrier_semaphore()
    reached = sorted({(axis, send[4] % RING[axis]) for axis, sends in plan().values() for send in sends})
    peers = [neighbour(axis, k) for axis, k in reached]
    peers += [f_dev(k) for k in range(1, n_f)]
    for peer in peers:
        pl.semaphore_signal(barrier, inc=1, device_id=peer, device_id_type=MESH)

    for ref in (hid, dg, du):
        ref[:, HP - LANE : HP] = jnp.zeros((rows, LANE), BF16)
    wrem[rest:LANE, :] = jnp.zeros((LANE - rest, D), BF16)
    wrem[LANE + rest : 2 * LANE, :] = jnp.zeros((LANE - rest, D), BF16)
    for key, ref in buf.items():
        if key[-1] == "pack":
            ref[...] = jnp.zeros_like(ref)

    blocks = [(lo, lo + 256) for lo in range(0, full, 256)] + [(full, hidden)]
    step_rows = rows // 2

    def products(lo, hi, r):
        if lo < full:
            return nt(xv[r, :], wgv[lo:hi, :]), nt(xv[r, :], wuv[lo:hi, :]), nt(cv[r, :], wdv[lo:hi, :])
        both = nt(xv[r, :], wrem[...])
        return both[:, 0:rest], both[:, LANE : LANE + rest], nt(cv[r, :], wdv[lo:hi, :])

    def terms(lo, hi, r, gate_pre, up_pre, back):
        gelu_value, gelu_slope = gelu_pair(gate_pre)
        hid[r, lo:hi] = (gelu_value * up_pre).astype(BF16)
        dg[r, lo:hi] = (back * up_pre * gelu_slope).astype(BF16)
        du[r, lo:hi] = (back * gelu_value).astype(BF16)

    row_blocks = [slice(lo, lo + step_rows) for lo in range(0, rows, step_rows)]
    taken = 0
    before = None
    for i, (lo, hi) in enumerate(blocks):
        count = 5 if i == 0 else 3
        for load in loads[taken : taken + count]:
            load.wait()
        taken += count
        now = []
        for j, r in enumerate(row_blocks):
            now.append(products(lo, hi, r))
            if before is not None:
                terms(*blocks[i - 1], r, *before[j])
        before = now
    for load in loads[taken:]:
        load.wait()

    slot_rows = [slice(e * seq, (e + 1) * seq) for e in range(SLOTS)]
    gram_x = [nt(xv[r, :], xv[r, :]) for r in slot_rows]
    gram_c = [nt(cv[r, :], cv[r, :]) for r in slot_rows]
    for j, r in enumerate(row_blocks):
        terms(*blocks[-1], r, *before[j])
    for e, r in enumerate(slot_rows):
        dge, due, he = dg[r, :], du[r, :], hid[r, :]
        prod = gram_x[e] * (nt(dge, dge) + nt(due, due)) + nt(he, he) * gram_c[e]
        part = prod[:, 0:LANE]
        for lo in range(LANE, seq, LANE):
            part = part + prod[:, lo : lo + LANE]
        nrm_send[8 * e : 8 * e + 8, :] = part.reshape(seq // 8, 8, LANE).sum(axis=0)

    pl.semaphore_wait(barrier, len(peers))

    sent = []

    def remote(src, dst, send_sem, recv_sem, dev):
        copy = pltpu.make_async_remote_copy(
            src_ref=src, dst_ref=dst, send_sem=send_sem, recv_sem=recv_sem, device_id=dev, device_id_type=MESH
        )
        copy.start()
        sent.append(copy)
        return copy

    norm_copies = [
        remote(nrm_send, nrm_recv.at[k - 1], nrm_ssem.at[k - 1], nrm_rsem.at[k - 1], f_dev(k))
        for k in range(1, n_f)
    ]

    def reorder(dst):
        for ox in range(NX):
            for oz in range(NZ):
                src_at = OWN * (NZ * ox + oz)
                dst_at = OWN * (NX * oz + ox)
                dst[dst_at : dst_at + OWN, :] = stage[src_at : src_at + OWN, :]

    turned = xv[...].T
    xt[...] = turned
    stage[...] = turned.astype(F32)
    reorder(perm)
    xt_z[...] = perm[...].astype(BF16)
    stage[...] = cv[...].T.astype(F32)
    reorder(perm)

    for copy in norm_copies:
        copy.wait_recv()
    total = nrm_send[...]
    for k in range(n_f - 1):
        total = total + nrm_recv[k]
    live = live_ref[0]
    factors = []
    for e in range(SLOTS):
        squared = jnp.sum(total[8 * e : 8 * e + 8, :], axis=(0, 1), keepdims=True)
        is_live = jnp.where(e < live, 1.0, 0.0).astype(F32)
        factors.append(is_live * bound / jnp.maximum(jnp.sqrt(jnp.maximum(squared, 0.0)), bound))

    matrix = {"gate": dg, "up": du, "down": hid}
    scaled = set()

    def right_side(src, lo, hi):
        if src != "down" and (src, lo) not in scaled:
            scaled.add((src, lo))
            for e in range(SLOTS):
                r = slice(e * seq, (e + 1) * seq)
                matrix[src][r, lo:hi] = (matrix[src][r, lo:hi].astype(F32) * factors[e]).astype(BF16)
        return matrix[src][:, lo:hi]

    def left_side(axis, src, k):
        n = XROWS if axis == "x" else ZROWS
        r = pl.ds(pl.multiple_of(at(axis, k) * n, n), n)
        if src != "down":
            return xt[r, :] if axis == "x" else xt_z[r, :]
        if k not in scaled:
            scaled.add(k)
            for e in range(SLOTS):
                c = slice(e * seq, (e + 1) * seq)
                ct_z[r, c] = (perm[r, c] * factors[e]).astype(BF16)
        return ct_z[r, :]

    def product(g, h, k):
        axis, halves, _ = GROUPS[g]
        parts = []
        for src, lo, hi in halves[h]:
            right = right_side(src, lo, hi)
            parts.append(nn(left_side(axis, src, k), right))
        return parts[0] if len(parts) == 1 else jnp.concatenate(parts, axis=1)

    routes = plan()
    copies = {}
    spot = {}
    numbers = {}
    for (g, phase), (ring, sends) in routes.items():
        used = [0, 0]
        row = 0
        packed = packed_rows(g)
        for i, (step, way, halves, owner, target, adds) in enumerate(sends):
            numbers[g, phase, i] = len(numbers)
            if phase == 1:
                spot[g, phase, i] = (used[halves[0]],)
                used[halves[0]] += 1
            else:
                n = sum(packed[h] for h in halves)
                spot[g, phase, i] = (row, n)
                row += n

    def received(g, phase, i, h):
        if phase == 1:
            return buf[g, h, "r1"][spot[g, phase, i][0]].astype(F32)
        row, _ = spot[g, phase, i]
        packed = packed_rows(g)
        for half in routes[g, phase][1][i][2]:
            if half == h:
                return buf[g, "r2"][row : row + packed[h], :].astype(F32)
            row += packed[half]

    def send(g, phase, step):
        ring, sends = routes[g, phase]
        packed = packed_rows(g)
        for i, (at_step, way, halves, owner, target, adds) in enumerate(sends):
            if at_step != step:
                continue
            values = []
            for h in halves:
                if phase == 1:
                    value = product(g, h, owner)
                else:
                    n = sum(packed)
                    first = pl.multiple_of(at(ring, owner) * n, n) + (packed[0] if h else 0)
                    value = buf[g, "pack"][pl.ds(pl.multiple_of(first, 16), packed[h]), :]
                values.append(value)
            for j in adds:
                copies[g, phase, j].wait_recv()
                for k, h in enumerate(halves):
                    if h in sends[j][2]:
                        values[k] = values[k] + received(g, phase, j, h)
            if phase == 1:
                h, slot = halves[0], spot[g, phase, i][0]
                src, dst = buf[g, h, "s1"].at[slot], buf[g, h, "r1"].at[slot]
                src[...] = values[0].astype(BF16)
            else:
                row, n = spot[g, phase, i]
                src, dst = buf[g, "s2"].at[pl.ds(row, n), :], buf[g, "r2"].at[pl.ds(row, n), :]
                for k, h in enumerate(halves):
                    buf[g, "s2"][row : row + packed[h], :] = values[k].astype(BF16)
                    row += packed[h]
            number = numbers[g, phase, i]
            copies[g, phase, i] = remote(src, dst, ssem.at[number], rsem.at[number], neighbour(ring, target))

    def arrived(g, phase, h, value):
        for i, (_, _, halves, owner, target, _) in enumerate(routes[g, phase][1]):
            if owner == target and h in halves:
                if (g, phase, i) not in waited:
                    waited.add((g, phase, i))
                    copies[g, phase, i].wait_recv()
                value = value + received(g, phase, i, h)
        return value

    waited = set()

    def close_first(g):
        axis, halves, _ = GROUPS[g]
        packed = packed_rows(g)
        for h, half in enumerate(halves):
            full_sum, pack = buf[g, h, "sum"], buf[g, "pack"]
            full_sum[...] = arrived(g, 1, h, product(g, h, 0))
            for o in range(NZ if axis == "x" else NX):
                for t in range(width_of(half) // LANE):
                    to = o * sum(packed) + (packed[0] if h else 0) + OWN * t
                    pack[to : to + OWN, :] = full_sum[OWN * o : OWN * o + OWN, LANE * t : LANE * t + LANE]

    out = {"gate": gate_ref, "up": up_ref, "down": down_ref}

    def close_second(g):
        axis, halves, _ = GROUPS[g]
        packed = packed_rows(g)
        n = sum(packed)
        pack = buf[g, "pack"]
        base = mine["z" if axis == "x" else "x"] * n
        for h, half in enumerate(halves):
            row = packed[0] if h else 0
            own = pack[pl.ds(pl.multiple_of(pl.multiple_of(base, n) + row, 16), packed[h]), :]
            buf_sum = fin.at[pl.ds(row, packed[h]), :]
            buf_sum[...] = arrived(g, 2, h, own)
            for src, lo, hi in half:
                for start in range(lo, hi, LANE):
                    width = min(LANE, hidden - start)
                    out[src][:, start : start + width] = fin[row : row + OWN, 0:width]
                    row += OWN

    for g, phase, step in ORDER:
        if phase == 0:
            close_first(g)
        elif phase == 3:
            close_second(g)
        else:
            send(g, phase, step)

    for copy in sent:
        copy.wait_send()


def add_noise(gate_ref, up_ref, down_ref, ng_ref, nu_ref, nd_ref, gate_out, up_out, down_out):
    gate_out[...] = gate_ref[...] + ng_ref[...]
    up_out[...] = up_ref[...] + nu_ref[...]
    down_out[...] = down_ref[...] + nd_ref[...]


def per_device(
    n_f, inputs, cotangent, gate_weight, up_weight, down_weight, live_counts, noise_gate, noise_up, noise_down
):
    rows = inputs.shape[0]
    seq = rows // SLOTS
    hidden = gate_weight.shape[1]
    full = hidden // 256 * 256
    bound = 0.1 * math.sqrt(SEQ * D * FF)
    any_spec = pl.BlockSpec(memory_space=pl.ANY)
    vmem = pl.BlockSpec(memory_space=pltpu.VMEM)
    dma = pltpu.SemaphoreType.DMA
    out = jax.ShapeDtypeStruct((OWN, hidden), F32)
    gate, up, down = pl.pallas_call(
        functools.partial(kernel, n_f, seq, hidden, bound),
        out_shape=(out, out, out),
        in_specs=[pl.BlockSpec(memory_space=pltpu.SMEM)] + [any_spec] * 5,
        out_specs=(vmem, vmem, vmem),
        scratch_shapes=[
            pltpu.VMEM((rows, D), BF16),
            pltpu.VMEM((rows, D), BF16),
            pltpu.VMEM((full, D), BF16),
            pltpu.VMEM((full, D), BF16),
            pltpu.VMEM((2 * LANE, D), BF16),
            pltpu.VMEM((hidden, D), BF16),
            pltpu.VMEM((rows, HP), BF16),
            pltpu.VMEM((rows, HP), BF16),
            pltpu.VMEM((rows, HP), BF16),
            pltpu.VMEM((D, rows), F32),
            pltpu.VMEM((D, rows), F32),
            pltpu.VMEM((D, rows), BF16),
            pltpu.VMEM((D, rows), BF16),
            pltpu.VMEM((D, rows), BF16),
            pltpu.VMEM((8 * SLOTS, LANE), F32),
            pltpu.VMEM((max(n_f - 1, 1), 8 * SLOTS, LANE), F32),
            pltpu.VMEM((max(sum(packed_rows(g)) for g in range(len(GROUPS))), LANE), F32),
            dma((2 + 3 * (full // 256) + 3,)),
            dma((max(n_f - 1, 1),)),
            dma((max(n_f - 1, 1),)),
            dma((total_sends(),)),
            dma((total_sends(),)),
        ]
        + [pltpu.VMEM(shape, dtype) for shape, dtype in scratch_plan().values()],
        compiler_params=pltpu.CompilerParams(
            collective_id=0, has_side_effects=True, vmem_limit_bytes=60 * 1024 * 1024
        ),
    )(live_counts, inputs, cotangent, gate_weight.T, up_weight.T, down_weight)
    gate, up, down = pl.pallas_call(
        add_noise,
        out_shape=(out, out, out),
        in_specs=[vmem] * 6,
        out_specs=(vmem, vmem, vmem),
    )(gate, up, down, noise_gate, noise_up, noise_down.T)
    return gate, up, down.T


def solution(mesh):
    in_specs = (
        P("dp", None),
        P("dp", None),
        P(None, "fsdp"),
        P(None, "fsdp"),
        P("fsdp", None),
        P("dp"),
        P("dp", "fsdp"),
        P("dp", "fsdp"),
        P("fsdp", "dp"),
    )
    out_specs = (P("dp", "fsdp"), P("dp", "fsdp"), P("fsdp", "dp"))
    return jax.shard_map(
        functools.partial(per_device, mesh.shape["fsdp"]),
        mesh=mesh, in_specs=in_specs, out_specs=out_specs, check_vma=False,
    )
```

```python
import functools
import math

import jax
import jax.numpy as jnp
from jax import lax
from jax.experimental import pallas as pl
from jax.experimental.pallas import tpu as pltpu
from jax.sharding import PartitionSpec as P

D = 1152
FF = 6912
SEQ = 256
SLOTS = 3
NX = 4
NZ = 8
OWN = D // (NX * NZ)
XROWS = D // NX
ZROWS = D // NZ
LANE = 128
F32 = jnp.float32
BF16 = jnp.bfloat16
MESH = pl.DeviceIdType.MESH

gelu_scale = 0.7978845608028654
gelu_cube = 0.044715

HP = 896
GROUPS = (
    ("z", ((("up", 512, 896),), (("down", 0, 256),)), "direct"),
    ("x", ((("gate", 0, 512),), (("gate", 512, 896), ("up", 0, 128),)), "chain"),
    ("z", ((("down", 256, 512),), (("down", 512, 896),)), "direct"),
    ("x", ((("up", 128, 384),), (("up", 384, 512),)), "tree"),
)
ORDER = (
    (2, 1, 0), (1, 1, 0), (2, 1, 1), (0, 1, 0), (0, 1, 1), (1, 1, 1), (2, 1, 2), (2, 1, 3),
    (0, 1, 2), (1, 1, 2), (0, 1, 3), (2, 1, 4), (2, 1, 5), (3, 1, 0), (0, 1, 4), (3, 1, 1),
    (0, 1, 5), (1, 0, 0), (2, 1, 6), (1, 2, 0), (3, 1, 2), (1, 2, 1), (0, 1, 6), (2, 0, 0),
    (2, 2, 0), (1, 2, 2), (1, 2, 3), (3, 0, 0), (3, 2, 0), (3, 2, 1), (0, 0, 0), (0, 2, 0),
    (1, 2, 4), (1, 2, 5), (2, 3, 0), (3, 2, 2), (1, 2, 6), (0, 3, 0), (3, 3, 0), (1, 3, 0),
)
RING = {"x": NX, "z": NZ}


def pad16(n):
    return (n + 15) // 16 * 16


def gelu_pair(values):
    square = values * values
    tangent = jnp.tanh(values * (gelu_scale + (gelu_scale * gelu_cube) * square))
    half_sum = 0.5 + 0.5 * tangent
    gelu_value = values * half_sum
    gelu_slope = half_sum + (0.5 * values) * (1.0 - tangent * tangent) * (
        gelu_scale + (3.0 * gelu_scale * gelu_cube) * square
    )
    return gelu_value, gelu_slope


def nt(a, b):
    return lax.dot_general(a, b, (((1,), (1,)), ((), ())), preferred_element_type=F32)


def nn(a, b):
    return lax.dot_general(a, b, (((1,), (0,)), ((), ())), preferred_element_type=F32)


def width_of(half):
    return sum(hi - lo for _, lo, hi in half)


def chain(axis):
    last, far = (3, 2) if axis == "x" else (7, 4)
    sends = []
    for step in range(last):
        for way in range(2):
            sign = 1 - 2 * way
            halves = ((way + step) % 2,)
            owner = sign * (far - (step + 1) // 2)
            sends.append((step, way, halves, owner, sign, (len(sends) - 4,) if step >= 2 else ()))
    return sends


def direct(axis):
    far = RING[axis] // 2
    sends = []
    for dist in range(far, 0, -1):
        for way in range(2):
            at = dist * (1 - 2 * way)
            sends.append((0, way, (way,) if dist == far else (0, 1), at, at, ()))
    return sends


def tree(axis):
    sends = []
    for way in range(2):
        sign = 1 - 2 * way
        sends.append((0, way, (way,), 4 * sign, 2 * sign, ()))
    for way in range(2):
        sign = 1 - 2 * way
        sends.append((0, way, (0, 1), 3 * sign, sign, ()))
    for way in range(2):
        sign = 1 - 2 * way
        sends.append((1, way, (0, 1), sign, sign, ()))
    for way in range(2):
        sign = 1 - 2 * way
        sends.append((2, way, (0, 1), 2 * sign, 2 * sign, (way, 2 + way)))
    return sends


SECOND = {"chain": chain, "direct": direct, "tree": tree}


def packed_rows(g):
    return [pad16(OWN * width_of(half) // LANE) for half in GROUPS[g][1]]


def plan():
    sends = {}
    for g, (axis, _, mode) in enumerate(GROUPS):
        other = "z" if axis == "x" else "x"
        sends[g, 1] = (axis, chain(axis))
        sends[g, 2] = (other, SECOND[mode](other))
    return sends


def scratch_plan():
    shapes = {}
    for g, (axis, halves, _) in enumerate(GROUPS):
        rows = XROWS if axis == "x" else ZROWS
        other = NZ if axis == "x" else NX
        first = RING[axis] - 1
        for h, half in enumerate(halves):
            width = width_of(half)
            shapes[g, h, "s1"] = ((first, rows, width), BF16)
            shapes[g, h, "r1"] = ((first, rows, width), BF16)
            shapes[g, h, "sum"] = ((rows, width), F32)
        packed = packed_rows(g)
        shapes[g, "pack"] = ((other * sum(packed), LANE), F32)
        total = sum(packed[h] for send in plan()[g, 2][1] for h in send[2])
        shapes[g, "s2"] = ((total, LANE), BF16)
        shapes[g, "r2"] = ((total, LANE), BF16)
    return shapes


def total_sends():
    return sum(len(sends) for _, sends in plan().values())


def kernel(
    n_f, seq, hidden, bound,
    live_ref, x_hbm, c_hbm, wg_hbm, wu_hbm, wd_hbm,
    gate_ref, up_ref, down_ref,
    xv, cv, wgv, wuv, wrem, wdv,
    hid, dg, du, gram_x,
    stage, perm, xt, xt_z, ct_z,
    nrm_send, nrm_recv,
    fin, load_sem, nrm_ssem, nrm_rsem, ssem, rsem,
    *group_refs,
):
    rows = SLOTS * seq
    dp = lax.axis_index("dp")
    fs = lax.axis_index("fsdp")
    mine = {"x": dp // NZ, "z": dp % NZ}
    buf = dict(zip(scratch_plan(), group_refs))

    def at(axis, k):
        return (mine[axis] + (k + RING[axis])) % RING[axis]

    def neighbour(axis, k):
        if axis == "x":
            return (at("x", k) * NZ + mine["z"], fs)
        return (mine["x"] * NZ + at("z", k), fs)

    def f_dev(k):
        return (dp, (fs + k) % n_f)

    full = hidden // 256 * 256
    rest = hidden - full
    pairs = [(x_hbm, xv)]
    for lo in range(0, full, 256):
        r = pl.ds(lo, 256)
        pairs += [(wg_hbm.at[r, :], wgv.at[r, :]), (wu_hbm.at[r, :], wuv.at[r, :])]
        if lo == 0:
            pairs.append((c_hbm, cv))
        pairs.append((wd_hbm.at[r, :], wdv.at[r, :]))
    r = pl.ds(full, rest)
    pairs.append((wg_hbm.at[r, :], wrem.at[pl.ds(0, rest), :]))
    pairs.append((wu_hbm.at[r, :], wrem.at[pl.ds(LANE, rest), :]))
    pairs.append((wd_hbm.at[r, :], wdv.at[r, :]))
    loads = [pltpu.make_async_copy(src, dst, load_sem.at[i]) for i, (src, dst) in enumerate(pairs)]
    for load in loads:
        load.start()

    barrier = pltpu.get_barrier_semaphore()
    reached = sorted({(axis, send[4] % RING[axis]) for axis, sends in plan().values() for send in sends})
    peers = [neighbour(axis, k) for axis, k in reached]
    peers += [f_dev(k) for k in range(1, n_f)]
    for peer in peers:
        pl.semaphore_signal(barrier, inc=1, device_id=peer, device_id_type=MESH)

    blocks = [(lo, lo + 256) for lo in range(0, full, 256)] + [(full, hidden)]
    step_rows = rows // 2

    def products(lo, hi, r):
        if lo < full:
            yield nt(xv[r, :], wgv[lo:hi, :])
            yield nt(xv[r, :], wuv[lo:hi, :])
        else:
            both = nt(xv[r, :], wrem[...])
            yield both[:, 0:rest]
            yield both[:, LANE : LANE + rest]
        yield nt(cv[r, :], wdv[lo:hi, :])

    def terms(lo, hi, r, gate_pre, up_pre, back):
        gelu_value, gelu_slope = gelu_pair(gate_pre)
        hid[r, lo:hi] = (gelu_value * up_pre).astype(BF16)
        dg[r, lo:hi] = (back * up_pre * gelu_slope).astype(BF16)
        du[r, lo:hi] = (back * gelu_value).astype(BF16)

    def reorder(dst):
        for ox in range(NX):
            for oz in range(NZ):
                src_at = OWN * (NZ * ox + oz)
                dst_at = OWN * (NX * oz + ox)
                dst[dst_at : dst_at + OWN, :] = stage[src_at : src_at + OWN, :]

    def turn(k):
        if k == 0:
            turned = xv[...].T
            xt[...] = turned
            stage[...] = turned.astype(F32)
        elif k == 1:
            reorder(perm)
        elif k == 2:
            xt_z[...] = perm[...].astype(BF16)
        elif k == 3:
            stage[...] = cv[...].T.astype(F32)
        elif k == 4:
            reorder(perm)

    row_blocks = [slice(lo, lo + step_rows) for lo in range(0, rows, step_rows)]
    taken = 0
    before = None
    loads[0].wait()
    taken = 1
    slot_rows = [slice(e * seq, (e + 1) * seq) for e in range(SLOTS)]
    for e, r in enumerate(slot_rows):
        gram_x[e] = nt(xv[r, :], xv[r, :])
    for ref in (hid, dg, du):
        ref[:, HP - LANE : HP] = jnp.zeros((rows, LANE), BF16)
    wrem[rest:LANE, :] = jnp.zeros((LANE - rest, D), BF16)
    wrem[LANE + rest : 2 * LANE, :] = jnp.zeros((LANE - rest, D), BF16)
    for key, ref in buf.items():
        if key[-1] == "pack":
            ref[...] = jnp.zeros_like(ref)
    for i, (lo, hi) in enumerate(blocks):
        count = 4 if i == 0 else 3
        for load in loads[taken : taken + count]:
            load.wait()
        taken += count
        now = []
        for j, r in enumerate(row_blocks):
            parts = []
            third = (r.stop - r.start) // 3
            for k, part in enumerate(products(lo, hi, r)):
                parts.append(part)
                if before is None:
                    turn(3 * j + k)
                else:
                    sub = slice(k * third, (k + 1) * third)
                    rows_now = slice(r.start + sub.start, r.start + sub.stop)
                    terms(*blocks[i - 1], rows_now, *(value[sub] for value in before[j]))
            now.append(parts)
        before = now
    for load in loads[taken:]:
        load.wait()

    gram_c = [nt(cv[r, :], cv[r, :]) for r in slot_rows]
    for j, r in enumerate(row_blocks):
        terms(*blocks[-1], r, *before[j])
    for e, r in enumerate(slot_rows):
        dge, due, he = dg[r, :], du[r, :], hid[r, :]
        prod = gram_x[e] * (nt(dge, dge) + nt(due, due)) + nt(he, he) * gram_c[e]
        part = prod[:, 0:LANE]
        for lo in range(LANE, seq, LANE):
            part = part + prod[:, lo : lo + LANE]
        nrm_send[8 * e : 8 * e + 8, :] = part.reshape(seq // 8, 8, LANE).sum(axis=0)

    pl.semaphore_wait(barrier, len(peers))

    sent = []

    def remote(src, dst, send_sem, recv_sem, dev):
        copy = pltpu.make_async_remote_copy(
            src_ref=src, dst_ref=dst, send_sem=send_sem, recv_sem=recv_sem, device_id=dev, device_id_type=MESH
        )
        copy.start()
        sent.append(copy)
        return copy

    norm_copies = [
        remote(nrm_send, nrm_recv.at[k - 1], nrm_ssem.at[k - 1], nrm_rsem.at[k - 1], f_dev(k))
        for k in range(1, n_f)
    ]

    for copy in norm_copies:
        copy.wait_recv()
    total = nrm_send[...]
    for k in range(n_f - 1):
        total = total + nrm_recv[k]
    live = live_ref[0]
    factors = []
    for e in range(SLOTS):
        squared = jnp.sum(total[8 * e : 8 * e + 8, :], axis=(0, 1), keepdims=True)
        is_live = jnp.where(e < live, 1.0, 0.0).astype(F32)
        factors.append(is_live * bound / jnp.maximum(jnp.sqrt(jnp.maximum(squared, 0.0)), bound))

    matrix = {"gate": dg, "up": du, "down": hid}
    scaled = set()

    def right_side(src, lo, hi):
        if src != "down" and (src, lo) not in scaled:
            scaled.add((src, lo))
            for e in range(SLOTS):
                r = slice(e * seq, (e + 1) * seq)
                matrix[src][r, lo:hi] = (matrix[src][r, lo:hi].astype(F32) * factors[e]).astype(BF16)
        return matrix[src][:, lo:hi]

    def left_side(axis, src, k):
        n = XROWS if axis == "x" else ZROWS
        r = pl.ds(pl.multiple_of(at(axis, k) * n, n), n)
        if src != "down":
            return xt[r, :] if axis == "x" else xt_z[r, :]
        if k not in scaled:
            scaled.add(k)
            for e in range(SLOTS):
                c = slice(e * seq, (e + 1) * seq)
                ct_z[r, c] = (perm[r, c] * factors[e]).astype(BF16)
        return ct_z[r, :]

    def product(g, h, k):
        axis, halves, _ = GROUPS[g]
        parts = []
        for src, lo, hi in halves[h]:
            right = right_side(src, lo, hi)
            parts.append(nn(left_side(axis, src, k), right))
        return parts[0] if len(parts) == 1 else jnp.concatenate(parts, axis=1)

    routes = plan()
    copies = {}
    spot = {}
    numbers = {}
    for (g, phase), (ring, sends) in routes.items():
        used = [0, 0]
        row = 0
        packed = packed_rows(g)
        for i, (step, way, halves, owner, target, adds) in enumerate(sends):
            numbers[g, phase, i] = len(numbers)
            if phase == 1:
                spot[g, phase, i] = (used[halves[0]],)
                used[halves[0]] += 1
            else:
                n = sum(packed[h] for h in halves)
                spot[g, phase, i] = (row, n)
                row += n

    def received(g, phase, i, h):
        if phase == 1:
            return buf[g, h, "r1"][spot[g, phase, i][0]].astype(F32)
        row, _ = spot[g, phase, i]
        packed = packed_rows(g)
        for half in routes[g, phase][1][i][2]:
            if half == h:
                return buf[g, "r2"][row : row + packed[h], :].astype(F32)
            row += packed[half]

    def send(g, phase, step):
        ring, sends = routes[g, phase]
        packed = packed_rows(g)
        for i, (at_step, way, halves, owner, target, adds) in enumerate(sends):
            if at_step != step:
                continue
            values = []
            for h in halves:
                if phase == 1:
                    value = product(g, h, owner)
                else:
                    n = sum(packed)
                    first = pl.multiple_of(at(ring, owner) * n, n) + (packed[0] if h else 0)
                    value = buf[g, "pack"][pl.ds(pl.multiple_of(first, 16), packed[h]), :]
                values.append(value)
            for j in adds:
                copies[g, phase, j].wait_recv()
                for k, h in enumerate(halves):
                    if h in sends[j][2]:
                        values[k] = values[k] + received(g, phase, j, h)
            if phase == 1:
                h, slot = halves[0], spot[g, phase, i][0]
                src, dst = buf[g, h, "s1"].at[slot], buf[g, h, "r1"].at[slot]
                src[...] = values[0].astype(BF16)
            else:
                row, n = spot[g, phase, i]
                src, dst = buf[g, "s2"].at[pl.ds(row, n), :], buf[g, "r2"].at[pl.ds(row, n), :]
                for k, h in enumerate(halves):
                    buf[g, "s2"][row : row + packed[h], :] = values[k].astype(BF16)
                    row += packed[h]
            number = numbers[g, phase, i]
            copies[g, phase, i] = remote(src, dst, ssem.at[number], rsem.at[number], neighbour(ring, target))

    def arrived(g, phase, h, value):
        for i, (_, _, halves, owner, target, _) in enumerate(routes[g, phase][1]):
            if owner == target and h in halves:
                if (g, phase, i) not in waited:
                    waited.add((g, phase, i))
                    copies[g, phase, i].wait_recv()
                value = value + received(g, phase, i, h)
        return value

    waited = set()

    def close_first(g):
        axis, halves, _ = GROUPS[g]
        packed = packed_rows(g)
        for h, half in enumerate(halves):
            full_sum, pack = buf[g, h, "sum"], buf[g, "pack"]
            full_sum[...] = arrived(g, 1, h, product(g, h, 0))
            for o in range(NZ if axis == "x" else NX):
                for t in range(width_of(half) // LANE):
                    to = o * sum(packed) + (packed[0] if h else 0) + OWN * t
                    pack[to : to + OWN, :] = full_sum[OWN * o : OWN * o + OWN, LANE * t : LANE * t + LANE]

    out = {"gate": gate_ref, "up": up_ref, "down": down_ref}

    def close_second(g):
        axis, halves, _ = GROUPS[g]
        packed = packed_rows(g)
        n = sum(packed)
        pack = buf[g, "pack"]
        base = mine["z" if axis == "x" else "x"] * n
        for h, half in enumerate(halves):
            row = packed[0] if h else 0
            own = pack[pl.ds(pl.multiple_of(pl.multiple_of(base, n) + row, 16), packed[h]), :]
            buf_sum = fin.at[pl.ds(row, packed[h]), :]
            buf_sum[...] = arrived(g, 2, h, own)
            for src, lo, hi in half:
                for start in range(lo, hi, LANE):
                    width = min(LANE, hidden - start)
                    out[src][:, start : start + width] = fin[row : row + OWN, 0:width]
                    row += OWN

    for g, phase, step in ORDER:
        if phase == 0:
            close_first(g)
        elif phase == 3:
            close_second(g)
        else:
            send(g, phase, step)

    for copy in sent:
        copy.wait_send()


def add_noise(gate_ref, up_ref, down_ref, ng_ref, nu_ref, nd_ref, gate_out, up_out, down_out):
    gate_out[...] = gate_ref[...] + ng_ref[...]
    up_out[...] = up_ref[...] + nu_ref[...]
    down_out[...] = down_ref[...] + nd_ref[...]


def per_device(
    n_f, inputs, cotangent, gate_weight, up_weight, down_weight, live_counts, noise_gate, noise_up, noise_down
):
    rows = inputs.shape[0]
    seq = rows // SLOTS
    hidden = gate_weight.shape[1]
    full = hidden // 256 * 256
    bound = 0.1 * math.sqrt(SEQ * D * FF)
    any_spec = pl.BlockSpec(memory_space=pl.ANY)
    vmem = pl.BlockSpec(memory_space=pltpu.VMEM)
    dma = pltpu.SemaphoreType.DMA
    out = jax.ShapeDtypeStruct((OWN, hidden), F32)
    held = pltpu.VMEM((OWN, hidden), F32)
    gate, up, down = pl.pallas_call(
        functools.partial(kernel, n_f, seq, hidden, bound),
        out_shape=(held, held, held),
        in_specs=[pl.BlockSpec(memory_space=pltpu.SMEM)] + [any_spec] * 5,
        out_specs=(vmem, vmem, vmem),
        scratch_shapes=[
            pltpu.VMEM((rows, D), BF16),
            pltpu.VMEM((rows, D), BF16),
            pltpu.VMEM((full, D), BF16),
            pltpu.VMEM((full, D), BF16),
            pltpu.VMEM((2 * LANE, D), BF16),
            pltpu.VMEM((hidden, D), BF16),
            pltpu.VMEM((rows, HP), BF16),
            pltpu.VMEM((rows, HP), BF16),
            pltpu.VMEM((rows, HP), BF16),
            pltpu.VMEM((SLOTS, seq, seq), F32),
            pltpu.VMEM((D, rows), F32),
            pltpu.VMEM((D, rows), F32),
            pltpu.VMEM((D, rows), BF16),
            pltpu.VMEM((D, rows), BF16),
            pltpu.VMEM((D, rows), BF16),
            pltpu.VMEM((8 * SLOTS, LANE), F32),
            pltpu.VMEM((max(n_f - 1, 1), 8 * SLOTS, LANE), F32),
            pltpu.VMEM((max(sum(packed_rows(g)) for g in range(len(GROUPS))), LANE), F32),
            dma((2 + 3 * (full // 256) + 3,)),
            dma((max(n_f - 1, 1),)),
            dma((max(n_f - 1, 1),)),
            dma((total_sends(),)),
            dma((total_sends(),)),
        ]
        + [pltpu.VMEM(shape, dtype) for shape, dtype in scratch_plan().values()],
        compiler_params=pltpu.CompilerParams(
            collective_id=0, has_side_effects=True, vmem_limit_bytes=60 * 1024 * 1024
        ),
    )(live_counts, inputs, cotangent, gate_weight.T, up_weight.T, down_weight)
    gate, up, down = pl.pallas_call(
        add_noise,
        out_shape=(out, out, out),
        in_specs=[vmem] * 6,
        out_specs=(vmem, vmem, vmem),
        compiler_params=pltpu.CompilerParams(vmem_limit_bytes=4 * 1024 * 1024),
    )(gate, up, down, noise_gate, noise_up, noise_down.T)
    return gate, up, down.T


def solution(mesh):
    in_specs = (
        P("dp", None),
        P("dp", None),
        P(None, "fsdp"),
        P(None, "fsdp"),
        P("fsdp", None),
        P("dp"),
        P("dp", "fsdp"),
        P("dp", "fsdp"),
        P("fsdp", "dp"),
    )
    out_specs = (P("dp", "fsdp"), P("dp", "fsdp"), P("fsdp", "dp"))
    return jax.shard_map(
        functools.partial(per_device, mesh.shape["fsdp"]),
        mesh=mesh, in_specs=in_specs, out_specs=out_specs, check_vma=False,
    )
```

```python
import functools
import math

import jax
import jax.numpy as jnp
from jax import lax
from jax.experimental import pallas as pl
from jax.experimental.pallas import tpu as pltpu
from jax.sharding import PartitionSpec as P

D = 1152
FF = 6912
SEQ = 256
SLOTS = 3
NX = 4
NZ = 8
OWN = D // (NX * NZ)
XROWS = D // NX
ZROWS = D // NZ
LANE = 128
F32 = jnp.float32
BF16 = jnp.bfloat16
MESH = pl.DeviceIdType.MESH

gelu_scale = 0.7978845608028654
gelu_cube = 0.044715

HIDDEN = FF // 8
HP = 896
REST = HIDDEN % LANE
GROUPS = (
    ("x", ((("gate", 0, 256),), (("gate", 640, 896),)), "chain"),
    ("x", ((("gate", 256, 512),), (("up", 640, 896),)), "chain"),
    ("x", ((("gate", 512, 640),), (("up", 0, 128),)), "tree"),
    ("x", ((("up", 128, 256),), (("up", 256, 384),)), "tree"),
    ("z", ((("down", 0, 640),), (("up", 384, 640), ("down", 640, 896),)), "direct"),
)
ORDER = (
    (0, 1, 0), (4, 1, 0), (0, 1, 1), (4, 1, 1), (1, 1, 0), (4, 1, 2), (0, 1, 2), (4, 1, 3),
    (1, 1, 1), (4, 1, 4), (1, 1, 2), (0, 0, 0), (0, 2, 0), (0, 2, 1), (3, 1, 0), (4, 1, 5),
    (3, 1, 1), (2, 1, 0), (1, 0, 0), (1, 2, 0), (1, 2, 1), (2, 1, 1), (0, 2, 2), (0, 2, 3),
    (4, 1, 6), (3, 1, 2), (2, 1, 2), (1, 2, 2), (1, 2, 3), (0, 2, 4), (0, 2, 5), (3, 0, 0),
    (3, 2, 0), (3, 2, 1), (4, 0, 0), (2, 0, 0), (2, 2, 0), (2, 2, 1), (4, 2, 0), (1, 2, 4),
    (1, 2, 5), (0, 2, 6), (3, 2, 2), (2, 2, 2), (1, 2, 6), (0, 3, 0), (3, 3, 0), (4, 3, 0),
    (1, 3, 0), (2, 3, 0),
)
RING = {"x": NX, "z": NZ}


def pad16(n):
    return (n + 15) // 16 * 16


def gelu_pair(values):
    square = values * values
    tangent = jnp.tanh(values * (gelu_scale + (gelu_scale * gelu_cube) * square))
    half_sum = 0.5 + 0.5 * tangent
    gelu_value = values * half_sum
    gelu_slope = half_sum + (0.5 * values) * (1.0 - tangent * tangent) * (
        gelu_scale + (3.0 * gelu_scale * gelu_cube) * square
    )
    return gelu_value, gelu_slope


def nt(a, b):
    return lax.dot_general(a, b, (((1,), (1,)), ((), ())), preferred_element_type=F32)


def nn(a, b):
    return lax.dot_general(a, b, (((1,), (0,)), ((), ())), preferred_element_type=F32)


def width_of(half):
    return sum(hi - lo for _, lo, hi in half)


def chain(axis):
    last, far = (3, 2) if axis == "x" else (7, 4)
    sends = []
    for step in range(last):
        for way in range(2):
            sign = 1 - 2 * way
            halves = ((way + step) % 2,)
            owner = sign * (far - (step + 1) // 2)
            sends.append((step, way, halves, owner, sign, (len(sends) - 4,) if step >= 2 else ()))
    return sends


def direct(axis):
    far = RING[axis] // 2
    sends = []
    for dist in range(far, 0, -1):
        for way in range(2):
            at = dist * (1 - 2 * way)
            sends.append((0, way, (way,) if dist == far else (0, 1), at, at, ()))
    return sends


def tree(axis):
    sends = []
    for way in range(2):
        sign = 1 - 2 * way
        sends.append((0, way, (way,), 4 * sign, 2 * sign, ()))
    for way in range(2):
        sign = 1 - 2 * way
        sends.append((0, way, (0, 1), 3 * sign, sign, ()))
    for way in range(2):
        sign = 1 - 2 * way
        sends.append((1, way, (0, 1), sign, sign, ()))
    for way in range(2):
        sign = 1 - 2 * way
        sends.append((2, way, (0, 1), 2 * sign, 2 * sign, (way, 2 + way)))
    return sends


SECOND = {"chain": chain, "direct": direct, "tree": tree}


def packed_rows(g):
    return [pad16(OWN * width_of(half) // LANE) for half in GROUPS[g][1]]


def plan():
    sends = {}
    for g, (axis, _, mode) in enumerate(GROUPS):
        other = "z" if axis == "x" else "x"
        sends[g, 1] = (axis, chain(axis))
        sends[g, 2] = (other, SECOND[mode](other))
    return sends


def tile_rows(axis, half):
    rows = XROWS if axis == "x" else ZROWS
    return [
        rows if at + LANE <= HIDDEN else rows * 7 // 9 for _, lo, hi in half for at in range(lo, hi, LANE)
    ]


def blocks_of(g, phase, halves):
    axis, all_halves, _ = GROUPS[g]
    if phase == 1:
        (h,) = halves
        return [((h, t), n) for t, n in enumerate(tile_rows(axis, all_halves[h]))]
    packed = packed_rows(g)
    return [((h,), packed[h]) for h in halves]


def scratch_plan():
    shapes = {}
    for g, (axis, halves, _) in enumerate(GROUPS):
        rows = XROWS if axis == "x" else ZROWS
        other = NZ if axis == "x" else NX
        for h, half in enumerate(halves):
            shapes[g, h, "sum"] = ((rows, width_of(half)), F32)
        shapes[g, "pack"] = ((other * sum(packed_rows(g)), LANE), F32)
        for phase in (1, 2):
            total = sum(n for send in plan()[g, phase][1] for _, n in blocks_of(g, phase, send[2]))
            shapes[g, f"s{phase}"] = ((total, LANE), BF16)
            shapes[g, f"r{phase}"] = ((total, LANE), BF16)
    return shapes


def lane_mask(shape, lo, hi):
    lane = lax.broadcasted_iota(jnp.int32, shape, 1)
    return (lane >= lo) & (lane < hi)


def fold(tile):
    rows = tile.shape[0]
    main = rows * 7 // 9
    rest = rows - main
    left = tile[main:rows, :]
    parts = []
    for j in range(3):
        moved = pltpu.roll(left, REST - 32 * j, 1)
        own = tile[rest * j : rest * (j + 1), :]
        parts.append(jnp.where(lane_mask(own.shape, REST, LANE), moved, own))
    parts.append(tile[3 * rest : main, :])
    return jnp.concatenate(parts, axis=0)


def unfold(tile):
    main = tile.shape[0]
    rows = main * 9 // 7
    rest = rows - main
    left = jnp.zeros((rest, LANE), F32)
    for j in range(3):
        moved = pltpu.roll(tile[rest * j : rest * (j + 1), :], 32 * j + LANE - REST, 1)
        left = jnp.where(lane_mask(left.shape, 32 * j, 32 * (j + 1)), moved, left)
    return jnp.concatenate([tile, left], axis=0)


def total_sends():
    return sum(len(sends) for _, sends in plan().values())


def kernel(
    n_f, seq, hidden, bound,
    live_ref, x_hbm, c_hbm, wg_hbm, wu_hbm, wd_hbm,
    gate_ref, up_ref, down_ref,
    xv, cv, wgv, wuv, wrem, wdv,
    hid, dg, du, gram_x,
    stage, perm, xt, xt_z, ct_z,
    nrm_send, nrm_recv,
    fin, load_sem, nrm_ssem, nrm_rsem, ssem, rsem,
    *group_refs,
):
    rows = SLOTS * seq
    dp = lax.axis_index("dp")
    fs = lax.axis_index("fsdp")
    mine = {"x": dp // NZ, "z": dp % NZ}
    buf = dict(zip(scratch_plan(), group_refs))

    def at(axis, k):
        return (mine[axis] + (k + RING[axis])) % RING[axis]

    def neighbour(axis, k):
        if axis == "x":
            return (at("x", k) * NZ + mine["z"], fs)
        return (mine["x"] * NZ + at("z", k), fs)

    def f_dev(k):
        return (dp, (fs + k) % n_f)

    full = hidden // 256 * 256
    rest = hidden - full
    pairs = [(x_hbm, xv)]
    for lo in range(0, full, 256):
        r = pl.ds(lo, 256)
        pairs += [(wg_hbm.at[r, :], wgv.at[r, :]), (wu_hbm.at[r, :], wuv.at[r, :])]
        if lo == 0:
            pairs.append((c_hbm, cv))
        pairs.append((wd_hbm.at[r, :], wdv.at[r, :]))
    r = pl.ds(full, rest)
    pairs.append((wg_hbm.at[r, :], wrem.at[pl.ds(0, rest), :]))
    pairs.append((wu_hbm.at[r, :], wrem.at[pl.ds(LANE, rest), :]))
    pairs.append((wd_hbm.at[r, :], wdv.at[r, :]))
    loads = [pltpu.make_async_copy(src, dst, load_sem.at[i]) for i, (src, dst) in enumerate(pairs)]
    for load in loads:
        load.start()

    barrier = pltpu.get_barrier_semaphore()
    reached = sorted({(axis, send[4] % RING[axis]) for axis, sends in plan().values() for send in sends})
    peers = [neighbour(axis, k) for axis, k in reached]
    peers += [f_dev(k) for k in range(1, n_f)]
    for peer in peers:
        pl.semaphore_signal(barrier, inc=1, device_id=peer, device_id_type=MESH)

    blocks = [(lo, lo + 256) for lo in range(0, full, 256)] + [(full, hidden)]
    step_rows = rows // 2

    def products(lo, hi, r):
        if lo < full:
            yield nt(xv[r, :], wgv[lo:hi, :])
            yield nt(xv[r, :], wuv[lo:hi, :])
        else:
            both = nt(xv[r, :], wrem[...])
            yield both[:, 0:rest]
            yield both[:, LANE : LANE + rest]
        yield nt(cv[r, :], wdv[lo:hi, :])

    def terms(lo, hi, r, gate_pre, up_pre, back):
        gelu_value, gelu_slope = gelu_pair(gate_pre)
        hid[r, lo:hi] = (gelu_value * up_pre).astype(BF16)
        dg[r, lo:hi] = (back * up_pre * gelu_slope).astype(BF16)
        du[r, lo:hi] = (back * gelu_value).astype(BF16)

    def reorder(dst):
        for ox in range(NX):
            for oz in range(NZ):
                src_at = OWN * (NZ * ox + oz)
                dst_at = OWN * (NX * oz + ox)
                dst[dst_at : dst_at + OWN, :] = stage[src_at : src_at + OWN, :]

    def turn(k):
        if k == 0:
            turned = xv[...].T
            xt[...] = turned
            stage[...] = turned.astype(F32)
        elif k == 1:
            reorder(perm)
        elif k == 2:
            xt_z[...] = perm[...].astype(BF16)
        elif k == 3:
            stage[...] = cv[...].T.astype(F32)
        elif k == 4:
            reorder(perm)

    row_blocks = [slice(lo, lo + step_rows) for lo in range(0, rows, step_rows)]
    taken = 0
    before = None
    loads[0].wait()
    taken = 1
    slot_rows = [slice(e * seq, (e + 1) * seq) for e in range(SLOTS)]
    for e, r in enumerate(slot_rows):
        gram_x[e] = nt(xv[r, :], xv[r, :])
    for ref in (hid, dg, du):
        ref[:, HP - LANE : HP] = jnp.zeros((rows, LANE), BF16)
    wrem[rest:LANE, :] = jnp.zeros((LANE - rest, D), BF16)
    wrem[LANE + rest : 2 * LANE, :] = jnp.zeros((LANE - rest, D), BF16)
    for key, ref in buf.items():
        if key[-1] == "pack":
            ref[...] = jnp.zeros_like(ref)
    for i, (lo, hi) in enumerate(blocks):
        count = 4 if i == 0 else 3
        for load in loads[taken : taken + count]:
            load.wait()
        taken += count
        now = []
        for j, r in enumerate(row_blocks):
            parts = []
            third = (r.stop - r.start) // 3
            for k, part in enumerate(products(lo, hi, r)):
                parts.append(part)
                if before is None:
                    turn(3 * j + k)
                else:
                    sub = slice(k * third, (k + 1) * third)
                    rows_now = slice(r.start + sub.start, r.start + sub.stop)
                    terms(*blocks[i - 1], rows_now, *(value[sub] for value in before[j]))
            now.append(parts)
        before = now
    for load in loads[taken:]:
        load.wait()

    gram_c = [nt(cv[r, :], cv[r, :]) for r in slot_rows]
    for j, r in enumerate(row_blocks):
        terms(*blocks[-1], r, *before[j])
    for e, r in enumerate(slot_rows):
        dge, due, he = dg[r, :], du[r, :], hid[r, :]
        prod = gram_x[e] * (nt(dge, dge) + nt(due, due)) + nt(he, he) * gram_c[e]
        part = prod[:, 0:LANE]
        for lo in range(LANE, seq, LANE):
            part = part + prod[:, lo : lo + LANE]
        nrm_send[8 * e : 8 * e + 8, :] = part.reshape(seq // 8, 8, LANE).sum(axis=0)

    pl.semaphore_wait(barrier, len(peers))

    sent = []

    def remote(src, dst, send_sem, recv_sem, dev):
        copy = pltpu.make_async_remote_copy(
            src_ref=src, dst_ref=dst, send_sem=send_sem, recv_sem=recv_sem, device_id=dev, device_id_type=MESH
        )
        copy.start()
        sent.append(copy)
        return copy

    norm_copies = [
        remote(nrm_send, nrm_recv.at[k - 1], nrm_ssem.at[k - 1], nrm_rsem.at[k - 1], f_dev(k))
        for k in range(1, n_f)
    ]

    for copy in norm_copies:
        copy.wait_recv()
    total = nrm_send[...]
    for k in range(n_f - 1):
        total = total + nrm_recv[k]
    live = live_ref[0]
    factors = []
    for e in range(SLOTS):
        squared = jnp.sum(total[8 * e : 8 * e + 8, :], axis=(0, 1), keepdims=True)
        is_live = jnp.where(e < live, 1.0, 0.0).astype(F32)
        factors.append(is_live * bound / jnp.maximum(jnp.sqrt(jnp.maximum(squared, 0.0)), bound))

    matrix = {"gate": dg, "up": du, "down": hid}
    scaled = set()

    def right_side(src, lo, hi):
        if src != "down" and (src, lo) not in scaled:
            scaled.add((src, lo))
            for e in range(SLOTS):
                r = slice(e * seq, (e + 1) * seq)
                matrix[src][r, lo:hi] = (matrix[src][r, lo:hi].astype(F32) * factors[e]).astype(BF16)
        return matrix[src][:, lo:hi]

    def left_side(axis, src, k):
        n = XROWS if axis == "x" else ZROWS
        r = pl.ds(pl.multiple_of(at(axis, k) * n, n), n)
        if src != "down":
            return xt[r, :] if axis == "x" else xt_z[r, :]
        if k not in scaled:
            scaled.add(k)
            for e in range(SLOTS):
                c = slice(e * seq, (e + 1) * seq)
                ct_z[r, c] = (perm[r, c] * factors[e]).astype(BF16)
        return ct_z[r, :]

    def product(g, h, k):
        axis, halves, _ = GROUPS[g]
        parts = []
        for src, lo, hi in halves[h]:
            right = right_side(src, lo, hi)
            parts.append(nn(left_side(axis, src, k), right))
        tiles = [part[:, at : at + LANE] for part in parts for at in range(0, part.shape[1], LANE)]
        return [
            tile if n == tile.shape[0] else fold(tile) for tile, n in zip(tiles, tile_rows(axis, halves[h]))
        ]

    routes = plan()
    copies = {}
    spot = {}
    numbers = {}
    for (g, phase), (ring, sends) in routes.items():
        row = 0
        for i, (_, _, halves, _, _, _) in enumerate(sends):
            numbers[g, phase, i] = len(numbers)
            n = sum(n for _, n in blocks_of(g, phase, halves))
            spot[g, phase, i] = (row, n)
            row += n

    def received(g, phase, i):
        row, _ = spot[g, phase, i]
        found = {}
        for key, n in blocks_of(g, phase, routes[g, phase][1][i][2]):
            found[key] = slice(row, row + n)
            row += n
        return {key: buf[g, f"r{phase}"][r, :].astype(F32) for key, r in found.items()}

    def send(g, phase, step):
        ring, sends = routes[g, phase]
        for i, (at_step, way, halves, owner, target, adds) in enumerate(sends):
            if at_step != step:
                continue
            blocks = blocks_of(g, phase, halves)
            if phase == 1:
                values = product(g, halves[0], owner)
            else:
                packed = packed_rows(g)
                n = sum(packed)
                values = []
                for h in halves:
                    first = pl.multiple_of(at(ring, owner) * n, n) + (packed[0] if h else 0)
                    values.append(buf[g, "pack"][pl.ds(pl.multiple_of(first, 16), packed[h]), :])
            for j in adds:
                copies[g, phase, j].wait_recv()
                came = received(g, phase, j)
                values = [v + came[key] if key in came else v for v, (key, _) in zip(values, blocks)]
            row, n = spot[g, phase, i]
            src, dst = (buf[g, f"{side}{phase}"].at[pl.ds(row, n), :] for side in "sr")
            for value, (_, rows_now) in zip(values, blocks):
                buf[g, f"s{phase}"][row : row + rows_now, :] = value.astype(BF16)
                row += rows_now
            number = numbers[g, phase, i]
            copies[g, phase, i] = remote(src, dst, ssem.at[number], rsem.at[number], neighbour(ring, target))

    def arrived(g, phase, h, values):
        for i, (_, _, halves, owner, target, _) in enumerate(routes[g, phase][1]):
            if owner == target and h in halves:
                if (g, phase, i) not in waited:
                    waited.add((g, phase, i))
                    copies[g, phase, i].wait_recv()
                came = received(g, phase, i)
                values = [v + came[key] for v, (key, _) in zip(values, blocks_of(g, phase, (h,)))]
        return values

    waited = set()

    def close_first(g):
        axis, halves, _ = GROUPS[g]
        packed = packed_rows(g)
        for h, half in enumerate(halves):
            full_sum, pack = buf[g, h, "sum"], buf[g, "pack"]
            for t, tile in enumerate(arrived(g, 1, h, product(g, h, 0))):
                if tile.shape[0] < full_sum.shape[0]:
                    tile = unfold(tile)
                full_sum[:, LANE * t : LANE * t + LANE] = tile
            for o in range(NZ if axis == "x" else NX):
                for t in range(width_of(half) // LANE):
                    to = o * sum(packed) + (packed[0] if h else 0) + OWN * t
                    pack[to : to + OWN, :] = full_sum[OWN * o : OWN * o + OWN, LANE * t : LANE * t + LANE]

    out = {"gate": gate_ref, "up": up_ref, "down": down_ref}

    def close_second(g):
        axis, halves, _ = GROUPS[g]
        packed = packed_rows(g)
        n = sum(packed)
        pack = buf[g, "pack"]
        base = mine["z" if axis == "x" else "x"] * n
        for h, half in enumerate(halves):
            row = packed[0] if h else 0
            own = pack[pl.ds(pl.multiple_of(pl.multiple_of(base, n) + row, 16), packed[h]), :]
            (fin[row : row + packed[h], :],) = arrived(g, 2, h, [own])
            for src, lo, hi in half:
                for start in range(lo, hi, LANE):
                    width = min(LANE, hidden - start)
                    out[src][:, start : start + width] = fin[row : row + OWN, 0:width]
                    row += OWN

    for g, phase, step in ORDER:
        if phase == 0:
            close_first(g)
        elif phase == 3:
            close_second(g)
        else:
            send(g, phase, step)

    for copy in sent:
        copy.wait_send()


def add_noise(gate_ref, up_ref, down_ref, ng_ref, nu_ref, nd_ref, gate_out, up_out, down_out):
    gate_out[...] = gate_ref[...] + ng_ref[...]
    up_out[...] = up_ref[...] + nu_ref[...]
    down_out[...] = down_ref[...] + nd_ref[...]


def per_device(
    n_f, inputs, cotangent, gate_weight, up_weight, down_weight, live_counts, noise_gate, noise_up, noise_down
):
    rows = inputs.shape[0]
    seq = rows // SLOTS
    hidden = gate_weight.shape[1]
    full = hidden // 256 * 256
    bound = 0.1 * math.sqrt(SEQ * D * FF)
    any_spec = pl.BlockSpec(memory_space=pl.ANY)
    vmem = pl.BlockSpec(memory_space=pltpu.VMEM)
    dma = pltpu.SemaphoreType.DMA
    out = jax.ShapeDtypeStruct((OWN, hidden), F32)
    held = pltpu.VMEM((OWN, hidden), F32)
    gate, up, down = pl.pallas_call(
        functools.partial(kernel, n_f, seq, hidden, bound),
        out_shape=(held, held, held),
        in_specs=[pl.BlockSpec(memory_space=pltpu.SMEM)] + [any_spec] * 5,
        out_specs=(vmem, vmem, vmem),
        scratch_shapes=[
            pltpu.VMEM((rows, D), BF16),
            pltpu.VMEM((rows, D), BF16),
            pltpu.VMEM((full, D), BF16),
            pltpu.VMEM((full, D), BF16),
            pltpu.VMEM((2 * LANE, D), BF16),
            pltpu.VMEM((hidden, D), BF16),
            pltpu.VMEM((rows, HP), BF16),
            pltpu.VMEM((rows, HP), BF16),
            pltpu.VMEM((rows, HP), BF16),
            pltpu.VMEM((SLOTS, seq, seq), F32),
            pltpu.VMEM((D, rows), F32),
            pltpu.VMEM((D, rows), F32),
            pltpu.VMEM((D, rows), BF16),
            pltpu.VMEM((D, rows), BF16),
            pltpu.VMEM((D, rows), BF16),
            pltpu.VMEM((8 * SLOTS, LANE), F32),
            pltpu.VMEM((max(n_f - 1, 1), 8 * SLOTS, LANE), F32),
            pltpu.VMEM((max(sum(packed_rows(g)) for g in range(len(GROUPS))), LANE), F32),
            dma((2 + 3 * (full // 256) + 3,)),
            dma((max(n_f - 1, 1),)),
            dma((max(n_f - 1, 1),)),
            dma((total_sends(),)),
            dma((total_sends(),)),
        ]
        + [pltpu.VMEM(shape, dtype) for shape, dtype in scratch_plan().values()],
        compiler_params=pltpu.CompilerParams(
            collective_id=0, has_side_effects=True, vmem_limit_bytes=60 * 1024 * 1024
        ),
    )(live_counts, inputs, cotangent, gate_weight.T, up_weight.T, down_weight)
    gate, up, down = pl.pallas_call(
        add_noise,
        out_shape=(out, out, out),
        in_specs=[vmem] * 6,
        out_specs=(vmem, vmem, vmem),
        compiler_params=pltpu.CompilerParams(vmem_limit_bytes=4 * 1024 * 1024),
    )(gate, up, down, noise_gate, noise_up, noise_down.T)
    return gate, up, down.T


def solution(mesh):
    in_specs = (
        P("dp", None),
        P("dp", None),
        P(None, "fsdp"),
        P(None, "fsdp"),
        P("fsdp", None),
        P("dp"),
        P("dp", "fsdp"),
        P("dp", "fsdp"),
        P("fsdp", "dp"),
    )
    out_specs = (P("dp", "fsdp"), P("dp", "fsdp"), P("fsdp", "dp"))
    return jax.shard_map(
        functools.partial(per_device, mesh.shape["fsdp"]),
        mesh=mesh, in_specs=in_specs, out_specs=out_specs, check_vma=False,
    )
```

```python
import functools
import math

import jax
import jax.numpy as jnp
from jax import lax
from jax.experimental import pallas as pl
from jax.experimental.pallas import tpu as pltpu
from jax.sharding import PartitionSpec as P

D = 1152
FF = 6912
SEQ = 256
SLOTS = 3
NX = 4
NZ = 8
OWN = D // (NX * NZ)
XROWS = D // NX
ZROWS = D // NZ
LANE = 128
F32 = jnp.float32
BF16 = jnp.bfloat16
MESH = pl.DeviceIdType.MESH

gelu_scale = 0.7978845608028654
gelu_cube = 0.044715

HIDDEN = FF // 8
HP = 896
REST = HIDDEN % LANE
GROUPS = (
    ("x", ((("gate", 0, 256),), (("gate", 640, 896),)), "chain"),
    ("x", ((("gate", 256, 512),), (("up", 640, 896),)), "chain"),
    ("x", ((("gate", 512, 640),), (("up", 0, 128),)), "tree"),
    ("x", ((("up", 128, 256),), (("up", 256, 384),)), "tree"),
    ("z", ((("down", 0, 640),), (("up", 384, 640), ("down", 640, 896),)), "direct"),
)
ORDER = (
    (0, 1, 0), (4, 1, 0), (0, 1, 1), (4, 1, 1), (1, 1, 0), (4, 1, 2), (0, 1, 2), (4, 1, 3),
    (1, 1, 1), (4, 1, 4), (1, 1, 2), (0, 0, 0), (0, 2, 0), (0, 2, 1), (3, 1, 0), (4, 1, 5),
    (3, 1, 1), (2, 1, 0), (1, 0, 0), (1, 2, 0), (1, 2, 1), (2, 1, 1), (0, 2, 2), (0, 2, 3),
    (4, 1, 6), (3, 1, 2), (2, 1, 2), (1, 2, 2), (1, 2, 3), (0, 2, 4), (0, 2, 5), (3, 0, 0),
    (3, 2, 0), (3, 2, 1), (4, 0, 0), (2, 0, 0), (2, 2, 0), (2, 2, 1), (4, 2, 0), (1, 2, 4),
    (1, 2, 5), (0, 2, 6), (3, 2, 2), (2, 2, 2), (1, 2, 6), (0, 3, 0), (3, 3, 0), (4, 3, 0),
    (1, 3, 0), (2, 3, 0),
)
RING = {"x": NX, "z": NZ}


def pad16(n):
    return (n + 15) // 16 * 16


def gelu_pair(values):
    square = values * values
    tangent = jnp.tanh(values * (gelu_scale + (gelu_scale * gelu_cube) * square))
    half_sum = 0.5 + 0.5 * tangent
    gelu_value = values * half_sum
    gelu_slope = half_sum + (0.5 * values) * (1.0 - tangent * tangent) * (
        gelu_scale + (3.0 * gelu_scale * gelu_cube) * square
    )
    return gelu_value, gelu_slope


def nt(a, b):
    return lax.dot_general(a, b, (((1,), (1,)), ((), ())), preferred_element_type=F32)


def nn(a, b):
    return lax.dot_general(a, b, (((1,), (0,)), ((), ())), preferred_element_type=F32)


def width_of(half):
    return sum(hi - lo for _, lo, hi in half)


def chain(axis):
    last, far = (3, 2) if axis == "x" else (7, 4)
    sends = []
    for step in range(last):
        for way in range(2):
            sign = 1 - 2 * way
            halves = ((way + step) % 2,)
            owner = sign * (far - (step + 1) // 2)
            sends.append((step, way, halves, owner, sign, (len(sends) - 4,) if step >= 2 else ()))
    return sends


def direct(axis):
    far = RING[axis] // 2
    sends = []
    for dist in range(far, 0, -1):
        for way in range(2):
            at = dist * (1 - 2 * way)
            sends.append((0, way, (way,) if dist == far else (0, 1), at, at, ()))
    return sends


def tree(axis):
    sends = []
    for way in range(2):
        sign = 1 - 2 * way
        sends.append((0, way, (way,), 4 * sign, 2 * sign, ()))
    for way in range(2):
        sign = 1 - 2 * way
        sends.append((0, way, (0, 1), 3 * sign, sign, ()))
    for way in range(2):
        sign = 1 - 2 * way
        sends.append((1, way, (0, 1), sign, sign, ()))
    for way in range(2):
        sign = 1 - 2 * way
        sends.append((2, way, (0, 1), 2 * sign, 2 * sign, (way, 2 + way)))
    return sends


SECOND = {"chain": chain, "direct": direct, "tree": tree}


def packed_rows(g):
    n = pad16(OWN * sum(width_of(half) for half in GROUPS[g][1]) // LANE)
    return [n // 32 * 16, n - n // 32 * 16]


def plan():
    sends = {}
    for g, (axis, _, mode) in enumerate(GROUPS):
        other = "z" if axis == "x" else "x"
        sends[g, 1] = (axis, chain(axis))
        sends[g, 2] = (other, SECOND[mode](other))
    return sends


def tile_rows(axis, half):
    rows = XROWS if axis == "x" else ZROWS
    return [
        rows if at + LANE <= HIDDEN else rows * 7 // 9 for _, lo, hi in half for at in range(lo, hi, LANE)
    ]


def blocks_of(g, phase, halves):
    axis, all_halves, _ = GROUPS[g]
    if phase == 1:
        (h,) = halves
        return [((h, t), n) for t, n in enumerate(tile_rows(axis, all_halves[h]))]
    packed = packed_rows(g)
    return [((h,), packed[h]) for h in halves]


def scratch_plan():
    shapes = {}
    for g, (axis, halves, _) in enumerate(GROUPS):
        rows = XROWS if axis == "x" else ZROWS
        other = NZ if axis == "x" else NX
        for h, half in enumerate(halves):
            shapes[g, h, "sum"] = ((rows, width_of(half)), F32)
        shapes[g, "pack"] = ((other * sum(packed_rows(g)), LANE), F32)
        for phase in (1, 2):
            total = sum(n for send in plan()[g, phase][1] for _, n in blocks_of(g, phase, send[2]))
            shapes[g, f"s{phase}"] = ((total, LANE), BF16)
            shapes[g, f"r{phase}"] = ((total, LANE), BF16)
    return shapes


def lane_mask(shape, lo, hi):
    lane = lax.broadcasted_iota(jnp.int32, shape, 1)
    return (lane >= lo) & (lane < hi)


def fold(tile):
    rows = tile.shape[0]
    main = rows * 7 // 9
    rest = rows - main
    left = tile[main:rows, :]
    parts = []
    for j in range(3):
        moved = pltpu.roll(left, REST - 32 * j, 1)
        own = tile[rest * j : rest * (j + 1), :]
        parts.append(jnp.where(lane_mask(own.shape, REST, LANE), moved, own))
    parts.append(tile[3 * rest : main, :])
    return jnp.concatenate(parts, axis=0)


def unfold(tile):
    main = tile.shape[0]
    rows = main * 9 // 7
    rest = rows - main
    left = jnp.zeros((rest, LANE), F32)
    for j in range(3):
        moved = pltpu.roll(tile[rest * j : rest * (j + 1), :], 32 * j + LANE - REST, 1)
        left = jnp.where(lane_mask(left.shape, 32 * j, 32 * (j + 1)), moved, left)
    return jnp.concatenate([tile, left], axis=0)


def total_sends():
    return sum(len(sends) for _, sends in plan().values())


def kernel(
    n_f, seq, hidden, bound,
    live_ref, x_hbm, c_hbm, wg_hbm, wu_hbm, wd_hbm,
    gate_ref, up_ref, down_ref,
    xv, cv, wgv, wuv, wrem, wdv,
    hid, dg, du, gram_x,
    stage, perm, xt, xt_z, ct_z,
    nrm_send, nrm_recv,
    fin, load_sem, nrm_ssem, nrm_rsem, ssem, rsem,
    *group_refs,
):
    rows = SLOTS * seq
    dp = lax.axis_index("dp")
    fs = lax.axis_index("fsdp")
    mine = {"x": dp // NZ, "z": dp % NZ}
    buf = dict(zip(scratch_plan(), group_refs))

    def at(axis, k):
        return (mine[axis] + (k + RING[axis])) % RING[axis]

    def neighbour(axis, k):
        if axis == "x":
            return (at("x", k) * NZ + mine["z"], fs)
        return (mine["x"] * NZ + at("z", k), fs)

    def f_dev(k):
        return (dp, (fs + k) % n_f)

    full = hidden // 256 * 256
    rest = hidden - full
    pairs = [(x_hbm, xv)]
    for lo in range(0, full, 256):
        r = pl.ds(lo, 256)
        pairs += [(wg_hbm.at[r, :], wgv.at[r, :]), (wu_hbm.at[r, :], wuv.at[r, :])]
        if lo == 0:
            pairs.append((c_hbm, cv))
        pairs.append((wd_hbm.at[r, :], wdv.at[r, :]))
    r = pl.ds(full, rest)
    pairs.append((wg_hbm.at[r, :], wrem.at[pl.ds(0, rest), :]))
    pairs.append((wu_hbm.at[r, :], wrem.at[pl.ds(LANE, rest), :]))
    pairs.append((wd_hbm.at[r, :], wdv.at[r, :]))
    loads = [pltpu.make_async_copy(src, dst, load_sem.at[i]) for i, (src, dst) in enumerate(pairs)]
    for load in loads:
        load.start()

    barrier = pltpu.get_barrier_semaphore()
    reached = sorted({(axis, send[4] % RING[axis]) for axis, sends in plan().values() for send in sends})
    peers = [neighbour(axis, k) for axis, k in reached]
    peers += [f_dev(k) for k in range(1, n_f)]
    for peer in peers:
        pl.semaphore_signal(barrier, inc=1, device_id=peer, device_id_type=MESH)

    blocks = [(lo, lo + 256) for lo in range(0, full, 256)] + [(full, hidden)]
    step_rows = rows // 2

    def products(lo, hi, r):
        if lo < full:
            yield nt(xv[r, :], wgv[lo:hi, :])
            yield nt(xv[r, :], wuv[lo:hi, :])
        else:
            both = nt(xv[r, :], wrem[...])
            yield both[:, 0:rest]
            yield both[:, LANE : LANE + rest]
        yield nt(cv[r, :], wdv[lo:hi, :])

    def terms(lo, hi, r, gate_pre, up_pre, back):
        gelu_value, gelu_slope = gelu_pair(gate_pre)
        hid[r, lo:hi] = (gelu_value * up_pre).astype(BF16)
        dg[r, lo:hi] = (back * up_pre * gelu_slope).astype(BF16)
        du[r, lo:hi] = (back * gelu_value).astype(BF16)

    def reorder(dst):
        for ox in range(NX):
            for oz in range(NZ):
                src_at = OWN * (NZ * ox + oz)
                dst_at = OWN * (NX * oz + ox)
                dst[dst_at : dst_at + OWN, :] = stage[src_at : src_at + OWN, :]

    def turn(k):
        if k == 0:
            turned = xv[...].T
            xt[...] = turned
            stage[...] = turned.astype(F32)
        elif k == 1:
            reorder(perm)
        elif k == 2:
            xt_z[...] = perm[...].astype(BF16)
        elif k == 3:
            stage[...] = cv[...].T.astype(F32)
        elif k == 4:
            reorder(perm)

    row_blocks = [slice(lo, lo + step_rows) for lo in range(0, rows, step_rows)]
    taken = 0
    before = None
    loads[0].wait()
    taken = 1
    slot_rows = [slice(e * seq, (e + 1) * seq) for e in range(SLOTS)]
    for e, r in enumerate(slot_rows):
        gram_x[e] = nt(xv[r, :], xv[r, :])
    nrm_send[...] = jnp.zeros_like(nrm_send)
    for ref in (hid, dg, du):
        ref[:, HP - LANE : HP] = jnp.zeros((rows, LANE), BF16)
    wrem[rest:LANE, :] = jnp.zeros((LANE - rest, D), BF16)
    wrem[LANE + rest : 2 * LANE, :] = jnp.zeros((LANE - rest, D), BF16)
    for key, ref in buf.items():
        if key[-1] == "pack":
            ref[...] = jnp.zeros_like(ref)
    for i, (lo, hi) in enumerate(blocks):
        count = 4 if i == 0 else 3
        for load in loads[taken : taken + count]:
            load.wait()
        taken += count
        now = []
        for j, r in enumerate(row_blocks):
            parts = []
            third = (r.stop - r.start) // 3
            for k, part in enumerate(products(lo, hi, r)):
                parts.append(part)
                if before is None:
                    turn(3 * j + k)
                else:
                    sub = slice(k * third, (k + 1) * third)
                    rows_now = slice(r.start + sub.start, r.start + sub.stop)
                    terms(*blocks[i - 1], rows_now, *(value[sub] for value in before[j]))
            now.append(parts)
        before = now
    for load in loads[taken:]:
        load.wait()

    gram_c = [nt(cv[r, :], cv[r, :]) for r in slot_rows]
    for j, r in enumerate(row_blocks):
        terms(*blocks[-1], r, *before[j])
    for e, r in enumerate(slot_rows):
        dge, due, he = dg[r, :], du[r, :], hid[r, :]
        prod = gram_x[e] * (nt(dge, dge) + nt(due, due)) + nt(he, he) * gram_c[e]
        part = prod[:, 0:LANE]
        for lo in range(LANE, seq, LANE):
            part = part + prod[:, lo : lo + LANE]
        nrm_send[e : e + 1, :] = jnp.sum(part, axis=0, keepdims=True)

    pl.semaphore_wait(barrier, len(peers))

    sent = []

    def remote(src, dst, send_sem, recv_sem, dev):
        copy = pltpu.make_async_remote_copy(
            src_ref=src, dst_ref=dst, send_sem=send_sem, recv_sem=recv_sem, device_id=dev, device_id_type=MESH
        )
        copy.start()
        sent.append(copy)
        return copy

    norm_copies = [
        remote(nrm_send, nrm_recv.at[k - 1], nrm_ssem.at[k - 1], nrm_rsem.at[k - 1], f_dev(k))
        for k in range(1, n_f)
    ]

    matrix = {"gate": dg, "up": du, "down": hid}
    routes = plan()
    slot_products = {}
    for first in ("x", "z"):
        g = next(g for g, phase, _ in ORDER if phase == 1 and GROUPS[g][0] == first)
        for step, _, (h,), owner, _, _ in routes[g, 1][1]:
            if step > 0:
                continue
            n = XROWS if first == "x" else ZROWS
            r = pl.ds(pl.multiple_of(at(first, owner) * n, n), n)
            parts = []
            for src, lo, hi in GROUPS[g][1][h]:
                for e in range(SLOTS):
                    c = slice(e * seq, (e + 1) * seq)
                    if src == "down":
                        left = perm[r, c].astype(BF16)
                    else:
                        left = xt[r, c] if first == "x" else xt_z[r, c]
                    parts.append(nn(left, matrix[src][c, lo:hi]))
            slot_products[g, h, owner] = parts

    for copy in norm_copies:
        copy.wait_recv()
    total = nrm_send[...]
    for k in range(n_f - 1):
        total = total + nrm_recv[k]
    live = live_ref[0]
    squared = jnp.sum(total, axis=1, keepdims=True)
    is_live = jnp.where(lax.broadcasted_iota(jnp.int32, squared.shape, 0) < live, 1.0, 0.0).astype(F32)
    factor = is_live * bound / jnp.maximum(jnp.sqrt(jnp.maximum(squared, 0.0)), bound)
    factors = [factor[e : e + 1, :] for e in range(SLOTS)]
    scaled = set()

    def right_side(src, lo, hi):
        if src != "down" and (src, lo) not in scaled:
            scaled.add((src, lo))
            for e in range(SLOTS):
                r = slice(e * seq, (e + 1) * seq)
                matrix[src][r, lo:hi] = (matrix[src][r, lo:hi].astype(F32) * factors[e]).astype(BF16)
        return matrix[src][:, lo:hi]

    def left_side(axis, src, k):
        n = XROWS if axis == "x" else ZROWS
        r = pl.ds(pl.multiple_of(at(axis, k) * n, n), n)
        if src != "down":
            return xt[r, :] if axis == "x" else xt_z[r, :]
        if k not in scaled:
            scaled.add(k)
            for e in range(SLOTS):
                c = slice(e * seq, (e + 1) * seq)
                ct_z[r, c] = (perm[r, c] * factors[e]).astype(BF16)
        return ct_z[r, :]

    def product(g, h, k):
        axis, halves, _ = GROUPS[g]
        parts = []
        early = slot_products.get((g, h, k))
        for i, (src, lo, hi) in enumerate(halves[h]):
            if early is None:
                right = right_side(src, lo, hi)
                parts.append(nn(left_side(axis, src, k), right))
            else:
                parts.append(sum(early[i * SLOTS + e] * factors[e] for e in range(SLOTS)))
        tiles = [part[:, at : at + LANE] for part in parts for at in range(0, part.shape[1], LANE)]
        return [
            tile if n == tile.shape[0] else fold(tile) for tile, n in zip(tiles, tile_rows(axis, halves[h]))
        ]

    copies = {}
    spot = {}
    numbers = {}
    for (g, phase), (ring, sends) in routes.items():
        row = 0
        for i, (_, _, halves, _, _, _) in enumerate(sends):
            numbers[g, phase, i] = len(numbers)
            n = sum(n for _, n in blocks_of(g, phase, halves))
            spot[g, phase, i] = (row, n)
            row += n

    def received(g, phase, i):
        row, _ = spot[g, phase, i]
        found = {}
        for key, n in blocks_of(g, phase, routes[g, phase][1][i][2]):
            found[key] = slice(row, row + n)
            row += n
        return {key: buf[g, f"r{phase}"][r, :].astype(F32) for key, r in found.items()}

    def send(g, phase, step):
        ring, sends = routes[g, phase]
        for i, (at_step, way, halves, owner, target, adds) in enumerate(sends):
            if at_step != step:
                continue
            blocks = blocks_of(g, phase, halves)
            if phase == 1:
                values = product(g, halves[0], owner)
            else:
                packed = packed_rows(g)
                n = sum(packed)
                values = []
                for h in halves:
                    first = pl.multiple_of(at(ring, owner) * n, n) + (packed[0] if h else 0)
                    values.append(buf[g, "pack"][pl.ds(pl.multiple_of(first, 16), packed[h]), :])
            for j in adds:
                copies[g, phase, j].wait_recv()
                came = received(g, phase, j)
                values = [v + came[key] if key in came else v for v, (key, _) in zip(values, blocks)]
            row, n = spot[g, phase, i]
            src, dst = (buf[g, f"{side}{phase}"].at[pl.ds(row, n), :] for side in "sr")
            for value, (_, rows_now) in zip(values, blocks):
                buf[g, f"s{phase}"][row : row + rows_now, :] = value.astype(BF16)
                row += rows_now
            number = numbers[g, phase, i]
            copies[g, phase, i] = remote(src, dst, ssem.at[number], rsem.at[number], neighbour(ring, target))

    def arrived(g, phase, h, values):
        for i, (_, _, halves, owner, target, _) in enumerate(routes[g, phase][1]):
            if owner == target and h in halves:
                if (g, phase, i) not in waited:
                    waited.add((g, phase, i))
                    copies[g, phase, i].wait_recv()
                came = received(g, phase, i)
                values = [v + came[key] for v, (key, _) in zip(values, blocks_of(g, phase, (h,)))]
        return values

    waited = set()

    def close_first(g):
        axis, halves, _ = GROUPS[g]
        packed = packed_rows(g)
        first = 0
        for h, half in enumerate(halves):
            full_sum, pack = buf[g, h, "sum"], buf[g, "pack"]
            for t, tile in enumerate(arrived(g, 1, h, product(g, h, 0))):
                if tile.shape[0] < full_sum.shape[0]:
                    tile = unfold(tile)
                full_sum[:, LANE * t : LANE * t + LANE] = tile
            for o in range(NZ if axis == "x" else NX):
                for t in range(width_of(half) // LANE):
                    to = o * sum(packed) + OWN * (first + t)
                    pack[to : to + OWN, :] = full_sum[OWN * o : OWN * o + OWN, LANE * t : LANE * t + LANE]
            first += width_of(half) // LANE

    out = {"gate": gate_ref, "up": up_ref, "down": down_ref}

    def close_second(g):
        axis, halves, _ = GROUPS[g]
        packed = packed_rows(g)
        n = sum(packed)
        pack = buf[g, "pack"]
        base = mine["z" if axis == "x" else "x"] * n
        for h in range(2):
            row = packed[0] if h else 0
            own = pack[pl.ds(pl.multiple_of(pl.multiple_of(base, n) + row, 16), packed[h]), :]
            (fin[row : row + packed[h], :],) = arrived(g, 2, h, [own])
        row = 0
        for src, lo, hi in halves[0] + halves[1]:
            for start in range(lo, hi, LANE):
                width = min(LANE, hidden - start)
                out[src][:, start : start + width] = fin[row : row + OWN, 0:width]
                row += OWN

    for g, phase, step in ORDER:
        if phase == 0:
            close_first(g)
        elif phase == 3:
            close_second(g)
        else:
            send(g, phase, step)

    for copy in sent:
        copy.wait_send()


def add_noise(gate_ref, up_ref, down_ref, ng_ref, nu_ref, nd_ref, gate_out, up_out, down_out):
    gate_out[...] = gate_ref[...] + ng_ref[...]
    up_out[...] = up_ref[...] + nu_ref[...]
    down_out[...] = down_ref[...] + nd_ref[...]


def per_device(
    n_f, inputs, cotangent, gate_weight, up_weight, down_weight, live_counts, noise_gate, noise_up, noise_down
):
    rows = inputs.shape[0]
    seq = rows // SLOTS
    hidden = gate_weight.shape[1]
    full = hidden // 256 * 256
    bound = 0.1 * math.sqrt(SEQ * D * FF)
    any_spec = pl.BlockSpec(memory_space=pl.ANY)
    vmem = pl.BlockSpec(memory_space=pltpu.VMEM)
    dma = pltpu.SemaphoreType.DMA
    out = jax.ShapeDtypeStruct((OWN, hidden), F32)
    held = pltpu.VMEM((OWN, hidden), F32)
    gate, up, down = pl.pallas_call(
        functools.partial(kernel, n_f, seq, hidden, bound),
        out_shape=(held, held, held),
        in_specs=[pl.BlockSpec(memory_space=pltpu.SMEM)] + [any_spec] * 5,
        out_specs=(vmem, vmem, vmem),
        scratch_shapes=[
            pltpu.VMEM((rows, D), BF16),
            pltpu.VMEM((rows, D), BF16),
            pltpu.VMEM((full, D), BF16),
            pltpu.VMEM((full, D), BF16),
            pltpu.VMEM((2 * LANE, D), BF16),
            pltpu.VMEM((hidden, D), BF16),
            pltpu.VMEM((rows, HP), BF16),
            pltpu.VMEM((rows, HP), BF16),
            pltpu.VMEM((rows, HP), BF16),
            pltpu.VMEM((SLOTS, seq, seq), F32),
            pltpu.VMEM((D, rows), F32),
            pltpu.VMEM((D, rows), F32),
            pltpu.VMEM((D, rows), BF16),
            pltpu.VMEM((D, rows), BF16),
            pltpu.VMEM((D, rows), BF16),
            pltpu.VMEM((8, LANE), F32),
            pltpu.VMEM((max(n_f - 1, 1), 8, LANE), F32),
            pltpu.VMEM((max(sum(packed_rows(g)) for g in range(len(GROUPS))), LANE), F32),
            dma((2 + 3 * (full // 256) + 3,)),
            dma((max(n_f - 1, 1),)),
            dma((max(n_f - 1, 1),)),
            dma((total_sends(),)),
            dma((total_sends(),)),
        ]
        + [pltpu.VMEM(shape, dtype) for shape, dtype in scratch_plan().values()],
        compiler_params=pltpu.CompilerParams(
            collective_id=0, has_side_effects=True, vmem_limit_bytes=60 * 1024 * 1024
        ),
    )(live_counts, inputs, cotangent, gate_weight.T, up_weight.T, down_weight)
    gate, up, down = pl.pallas_call(
        add_noise,
        out_shape=(out, out, out),
        in_specs=[vmem] * 6,
        out_specs=(vmem, vmem, vmem),
        compiler_params=pltpu.CompilerParams(vmem_limit_bytes=4 * 1024 * 1024),
    )(gate, up, down, noise_gate, noise_up, noise_down.T)
    return gate, up, down.T


def solution(mesh):
    in_specs = (
        P("dp", None),
        P("dp", None),
        P(None, "fsdp"),
        P(None, "fsdp"),
        P("fsdp", None),
        P("dp"),
        P("dp", "fsdp"),
        P("dp", "fsdp"),
        P("fsdp", "dp"),
    )
    out_specs = (P("dp", "fsdp"), P("dp", "fsdp"), P("fsdp", "dp"))
    return jax.shard_map(
        functools.partial(per_device, mesh.shape["fsdp"]),
        mesh=mesh, in_specs=in_specs, out_specs=out_specs, check_vma=False,
    )
```

```python
import functools
import math

import jax
import jax.numpy as jnp
from jax import lax
from jax.experimental import pallas as pl
from jax.experimental.pallas import tpu as pltpu
from jax.sharding import PartitionSpec as P

D = 1152
FF = 6912
SEQ = 256
SLOTS = 3
NX = 4
NZ = 8
OWN = D // (NX * NZ)
XROWS = D // NX
ZROWS = D // NZ
LANE = 128
F32 = jnp.float32
BF16 = jnp.bfloat16
MESH = pl.DeviceIdType.MESH

gelu_scale = 0.7978845608028654
gelu_cube = 0.044715

HIDDEN = FF // 8
HP = 896
REST = HIDDEN % LANE
GROUPS = (
    ("x", ((("gate", 0, 256),), (("gate", 640, 896),)), "chain"),
    ("x", ((("gate", 256, 512),), (("up", 640, 896),)), "chain"),
    ("x", ((("gate", 512, 640),), (("up", 0, 128),)), "tree"),
    ("x", ((("up", 128, 256),), (("up", 256, 384),)), "tree"),
    ("z", ((("down", 0, 640),), (("up", 384, 640), ("down", 640, 896),)), "direct"),
)
ORDER = (
    (4, 1, 0), (0, 1, 0), (0, 1, 1), (4, 1, 1), (1, 1, 0), (4, 1, 2), (0, 1, 2), (4, 1, 3),
    (1, 1, 1), (4, 1, 4), (1, 1, 2), (0, 0, 0), (0, 2, 0), (0, 2, 1), (3, 1, 0), (4, 1, 5),
    (3, 1, 1), (2, 1, 0), (1, 0, 0), (1, 2, 0), (1, 2, 1), (2, 1, 1), (0, 2, 2), (0, 2, 3),
    (4, 1, 6), (3, 1, 2), (2, 1, 2), (1, 2, 2), (1, 2, 3), (0, 2, 4), (0, 2, 5), (3, 0, 0),
    (3, 2, 0), (3, 2, 1), (4, 0, 0), (2, 0, 0), (2, 2, 0), (2, 2, 1), (4, 2, 0), (1, 2, 4),
    (1, 2, 5), (0, 2, 6), (3, 2, 2), (2, 2, 2), (1, 2, 6), (0, 3, 0), (3, 3, 0), (4, 3, 0),
    (1, 3, 0), (2, 3, 0),
)
RING = {"x": NX, "z": NZ}


def pad16(n):
    return (n + 15) // 16 * 16


def gelu_pair(values):
    square = values * values
    tangent = jnp.tanh(values * (gelu_scale + (gelu_scale * gelu_cube) * square))
    half_sum = 0.5 + 0.5 * tangent
    gelu_value = values * half_sum
    gelu_slope = half_sum + (0.5 * values) * (1.0 - tangent * tangent) * (
        gelu_scale + (3.0 * gelu_scale * gelu_cube) * square
    )
    return gelu_value, gelu_slope


def nt(a, b):
    return lax.dot_general(a, b, (((1,), (1,)), ((), ())), preferred_element_type=F32)


def nn(a, b):
    return lax.dot_general(a, b, (((1,), (0,)), ((), ())), preferred_element_type=F32)


def width_of(half):
    return sum(hi - lo for _, lo, hi in half)


def chain(axis):
    last, far = (3, 2) if axis == "x" else (7, 4)
    sends = []
    for step in range(last):
        for way in range(2):
            sign = 1 - 2 * way
            halves = ((way + step) % 2,)
            owner = sign * (far - (step + 1) // 2)
            sends.append((step, way, halves, owner, sign, (len(sends) - 4,) if step >= 2 else ()))
    return sends


def direct(axis):
    far = RING[axis] // 2
    sends = []
    for dist in range(far, 0, -1):
        for way in range(2):
            at = dist * (1 - 2 * way)
            sends.append((0, way, (way,) if dist == far else (0, 1), at, at, ()))
    return sends


def tree(axis):
    sends = []
    for way in range(2):
        sign = 1 - 2 * way
        sends.append((0, way, (way,), 4 * sign, 2 * sign, ()))
    for way in range(2):
        sign = 1 - 2 * way
        sends.append((0, way, (0, 1), 3 * sign, sign, ()))
    for way in range(2):
        sign = 1 - 2 * way
        sends.append((1, way, (0, 1), sign, sign, ()))
    for way in range(2):
        sign = 1 - 2 * way
        sends.append((2, way, (0, 1), 2 * sign, 2 * sign, (way, 2 + way)))
    return sends


SECOND = {"chain": chain, "direct": direct, "tree": tree}


def packed_rows(g):
    n = pad16(OWN * sum(width_of(half) for half in GROUPS[g][1]) // LANE)
    return [n // 32 * 16, n - n // 32 * 16]


def plan():
    sends = {}
    for g, (axis, _, mode) in enumerate(GROUPS):
        other = "z" if axis == "x" else "x"
        sends[g, 1] = (axis, chain(axis))
        sends[g, 2] = (other, SECOND[mode](other))
    return sends


def tile_rows(axis, half):
    rows = XROWS if axis == "x" else ZROWS
    return [
        rows if at + LANE <= HIDDEN else rows * 7 // 9 for _, lo, hi in half for at in range(lo, hi, LANE)
    ]


def blocks_of(g, phase, halves):
    axis, all_halves, _ = GROUPS[g]
    if phase == 1:
        (h,) = halves
        return [((h, t), n) for t, n in enumerate(tile_rows(axis, all_halves[h]))]
    packed = packed_rows(g)
    return [((h,), packed[h]) for h in halves]


def scratch_plan():
    shapes = {}
    for g, (axis, halves, _) in enumerate(GROUPS):
        rows = XROWS if axis == "x" else ZROWS
        other = NZ if axis == "x" else NX
        for h, half in enumerate(halves):
            shapes[g, h, "sum"] = ((rows, width_of(half)), F32)
        shapes[g, "pack"] = ((other * sum(packed_rows(g)), LANE), F32)
        for phase in (1, 2):
            total = sum(n for send in plan()[g, phase][1] for _, n in blocks_of(g, phase, send[2]))
            shapes[g, f"s{phase}"] = ((total, LANE), BF16)
            shapes[g, f"r{phase}"] = ((total, LANE), BF16)
    return shapes


def lane_mask(shape, lo, hi):
    lane = lax.broadcasted_iota(jnp.int32, shape, 1)
    return (lane >= lo) & (lane < hi)


def fold(tile):
    rows = tile.shape[0]
    main = rows * 7 // 9
    rest = rows - main
    left = tile[main:rows, :]
    parts = []
    for j in range(3):
        moved = pltpu.roll(left, REST - 32 * j, 1)
        own = tile[rest * j : rest * (j + 1), :]
        parts.append(jnp.where(lane_mask(own.shape, REST, LANE), moved, own))
    parts.append(tile[3 * rest : main, :])
    return jnp.concatenate(parts, axis=0)


def unfold(tile):
    main = tile.shape[0]
    rows = main * 9 // 7
    rest = rows - main
    left = jnp.zeros((rest, LANE), F32)
    for j in range(3):
        moved = pltpu.roll(tile[rest * j : rest * (j + 1), :], 32 * j + LANE - REST, 1)
        left = jnp.where(lane_mask(left.shape, 32 * j, 32 * (j + 1)), moved, left)
    return jnp.concatenate([tile, left], axis=0)


def total_sends():
    return sum(len(sends) for _, sends in plan().values())


def kernel(
    n_f, seq, hidden, bound,
    live_ref, x_hbm, c_hbm, wg_hbm, wu_hbm, wd_hbm,
    gate_ref, up_ref, down_ref,
    xv, cv, wgv, wuv, wrem, wdv,
    hid, dg, du, gram_x,
    stage, perm, xt, xt_z, ct_z,
    nrm_send, nrm_recv,
    fin, load_sem, nrm_ssem, nrm_rsem, ssem, rsem,
    *group_refs,
):
    rows = SLOTS * seq
    dp = lax.axis_index("dp")
    fs = lax.axis_index("fsdp")
    mine = {"x": dp // NZ, "z": dp % NZ}
    buf = dict(zip(scratch_plan(), group_refs))

    def at(axis, k):
        return (mine[axis] + (k + RING[axis])) % RING[axis]

    def neighbour(axis, k):
        if axis == "x":
            return (at("x", k) * NZ + mine["z"], fs)
        return (mine["x"] * NZ + at("z", k), fs)

    def f_dev(k):
        return (dp, (fs + k) % n_f)

    full = hidden // 256 * 256
    rest = hidden - full
    pairs = [(x_hbm, xv)]
    for lo in range(0, full, 256):
        r = pl.ds(lo, 256)
        pairs += [(wg_hbm.at[r, :], wgv.at[r, :]), (wu_hbm.at[r, :], wuv.at[r, :])]
        if lo == 0:
            pairs.append((c_hbm, cv))
        pairs.append((wd_hbm.at[r, :], wdv.at[r, :]))
    r = pl.ds(full, rest)
    pairs.append((wg_hbm.at[r, :], wrem.at[pl.ds(0, rest), :]))
    pairs.append((wu_hbm.at[r, :], wrem.at[pl.ds(LANE, rest), :]))
    pairs.append((wd_hbm.at[r, :], wdv.at[r, :]))
    loads = [pltpu.make_async_copy(src, dst, load_sem.at[i]) for i, (src, dst) in enumerate(pairs)]
    for load in loads:
        load.start()

    barrier = pltpu.get_barrier_semaphore()
    reached = sorted({(axis, send[4] % RING[axis]) for axis, sends in plan().values() for send in sends})
    peers = [neighbour(axis, k) for axis, k in reached]
    peers += [f_dev(k) for k in range(1, n_f)]
    for peer in peers:
        pl.semaphore_signal(barrier, inc=1, device_id=peer, device_id_type=MESH)

    blocks = [(lo, lo + 256) for lo in range(0, full, 256)] + [(full, hidden)]
    step_rows = rows // 2

    def products(lo, hi, r):
        if lo < full:
            yield nt(xv[r, :], wgv[lo:hi, :])
            yield nt(xv[r, :], wuv[lo:hi, :])
        else:
            both = nt(xv[r, :], wrem[...])
            yield both[:, 0:rest]
            yield both[:, LANE : LANE + rest]
        yield nt(cv[r, :], wdv[lo:hi, :])

    def terms(lo, hi, r, gate_pre, up_pre, back):
        gelu_value, gelu_slope = gelu_pair(gate_pre)
        hid[r, lo:hi] = (gelu_value * up_pre).astype(BF16)
        dg[r, lo:hi] = (back * up_pre * gelu_slope).astype(BF16)
        du[r, lo:hi] = (back * gelu_value).astype(BF16)

    def reorder(dst):
        for ox in range(NX):
            for oz in range(NZ):
                src_at = OWN * (NZ * ox + oz)
                dst_at = OWN * (NX * oz + ox)
                dst[dst_at : dst_at + OWN, :] = stage[src_at : src_at + OWN, :]

    def turn(k):
        if k == 0:
            turned = xv[...].T
            xt[...] = turned
            stage[...] = turned.astype(F32)
        elif k == 1:
            reorder(perm)
        elif k == 2:
            xt_z[...] = perm[...].astype(BF16)
        elif k == 3:
            stage[...] = cv[...].T.astype(F32)
        elif k == 4:
            reorder(perm)

    row_blocks = [slice(lo, lo + step_rows) for lo in range(0, rows, step_rows)]
    taken = 0
    before = None
    loads[0].wait()
    taken = 1
    slot_rows = [slice(e * seq, (e + 1) * seq) for e in range(SLOTS)]
    for e, r in enumerate(slot_rows):
        gram_x[e] = nt(xv[r, :], xv[r, :])
    nrm_send[...] = jnp.zeros_like(nrm_send)
    for ref in (hid, dg, du):
        ref[:, HP - LANE : HP] = jnp.zeros((rows, LANE), BF16)
    wrem[rest:LANE, :] = jnp.zeros((LANE - rest, D), BF16)
    wrem[LANE + rest : 2 * LANE, :] = jnp.zeros((LANE - rest, D), BF16)
    for key, ref in buf.items():
        if key[-1] == "pack":
            ref[...] = jnp.zeros_like(ref)
    for i, (lo, hi) in enumerate(blocks):
        count = 4 if i == 0 else 3
        for load in loads[taken : taken + count]:
            load.wait()
        taken += count
        now = []
        for j, r in enumerate(row_blocks):
            parts = []
            third = (r.stop - r.start) // 3
            for k, part in enumerate(products(lo, hi, r)):
                parts.append(part)
                if before is None:
                    turn(3 * j + k)
                else:
                    sub = slice(k * third, (k + 1) * third)
                    rows_now = slice(r.start + sub.start, r.start + sub.stop)
                    terms(*blocks[i - 1], rows_now, *(value[sub] for value in before[j]))
            now.append(parts)
        before = now
    for load in loads[taken:]:
        load.wait()

    gram_c = [nt(cv[r, :], cv[r, :]) for r in slot_rows]
    for j, r in enumerate(row_blocks):
        terms(*blocks[-1], r, *before[j])
    for e, r in enumerate(slot_rows):
        dge, due, he = dg[r, :], du[r, :], hid[r, :]
        prod = gram_x[e] * (nt(dge, dge) + nt(due, due)) + nt(he, he) * gram_c[e]
        part = prod[:, 0:LANE]
        for lo in range(LANE, seq, LANE):
            part = part + prod[:, lo : lo + LANE]
        nrm_send[e : e + 1, :] = jnp.sum(part, axis=0, keepdims=True)

    pl.semaphore_wait(barrier, len(peers))

    sent = []

    def remote(src, dst, send_sem, recv_sem, dev):
        copy = pltpu.make_async_remote_copy(
            src_ref=src, dst_ref=dst, send_sem=send_sem, recv_sem=recv_sem, device_id=dev, device_id_type=MESH
        )
        copy.start()
        sent.append(copy)
        return copy

    norm_copies = [
        remote(nrm_send, nrm_recv.at[k - 1], nrm_ssem.at[k - 1], nrm_rsem.at[k - 1], f_dev(k))
        for k in range(1, n_f)
    ]

    matrix = {"gate": dg, "up": du, "down": hid}
    routes = plan()
    slot_products = {}
    for first in ("x", "z"):
        g = next(g for g, phase, _ in ORDER if phase == 1 and GROUPS[g][0] == first)
        for step, _, (h,), owner, _, _ in routes[g, 1][1]:
            if step > 0:
                continue
            n = XROWS if first == "x" else ZROWS
            r = pl.ds(pl.multiple_of(at(first, owner) * n, n), n)
            parts = []
            for src, lo, hi in GROUPS[g][1][h]:
                for e in range(SLOTS):
                    c = slice(e * seq, (e + 1) * seq)
                    if src == "down":
                        left = perm[r, c].astype(BF16)
                    else:
                        left = xt[r, c] if first == "x" else xt_z[r, c]
                    parts.append(nn(left, matrix[src][c, lo:hi]))
            slot_products[g, h, owner] = parts

    for copy in norm_copies:
        copy.wait_recv()
    total = nrm_send[...]
    for k in range(n_f - 1):
        total = total + nrm_recv[k]
    live = live_ref[0]
    squared = jnp.sum(total, axis=1, keepdims=True)
    is_live = jnp.where(lax.broadcasted_iota(jnp.int32, squared.shape, 0) < live, 1.0, 0.0).astype(F32)
    factor = is_live * bound / jnp.maximum(jnp.sqrt(jnp.maximum(squared, 0.0)), bound)
    factors = [factor[e : e + 1, :] for e in range(SLOTS)]
    scaled = set()

    def right_side(src, lo, hi):
        if src != "down" and (src, lo) not in scaled:
            scaled.add((src, lo))
            for e in range(SLOTS):
                r = slice(e * seq, (e + 1) * seq)
                matrix[src][r, lo:hi] = (matrix[src][r, lo:hi].astype(F32) * factors[e]).astype(BF16)
        return matrix[src][:, lo:hi]

    def left_side(axis, src, k):
        n = XROWS if axis == "x" else ZROWS
        r = pl.ds(pl.multiple_of(at(axis, k) * n, n), n)
        if src != "down":
            return xt[r, :] if axis == "x" else xt_z[r, :]
        if k not in scaled:
            scaled.add(k)
            for e in range(SLOTS):
                c = slice(e * seq, (e + 1) * seq)
                ct_z[r, c] = (perm[r, c] * factors[e]).astype(BF16)
        return ct_z[r, :]

    def product(g, h, k):
        axis, halves, _ = GROUPS[g]
        parts = []
        early = slot_products.get((g, h, k))
        for i, (src, lo, hi) in enumerate(halves[h]):
            if early is None:
                right = right_side(src, lo, hi)
                parts.append(nn(left_side(axis, src, k), right))
            else:
                parts.append(sum(early[i * SLOTS + e] * factors[e] for e in range(SLOTS)))
        tiles = [part[:, at : at + LANE] for part in parts for at in range(0, part.shape[1], LANE)]
        return [
            tile if n == tile.shape[0] else fold(tile) for tile, n in zip(tiles, tile_rows(axis, halves[h]))
        ]

    copies = {}
    spot = {}
    numbers = {}
    for (g, phase), (ring, sends) in routes.items():
        row = 0
        for i, (_, _, halves, _, _, _) in enumerate(sends):
            numbers[g, phase, i] = len(numbers)
            n = sum(n for _, n in blocks_of(g, phase, halves))
            spot[g, phase, i] = (row, n)
            row += n

    def received(g, phase, i):
        row, _ = spot[g, phase, i]
        found = {}
        for key, n in blocks_of(g, phase, routes[g, phase][1][i][2]):
            found[key] = slice(row, row + n)
            row += n
        return {key: buf[g, f"r{phase}"][r, :].astype(F32) for key, r in found.items()}

    def send(g, phase, step):
        ring, sends = routes[g, phase]
        own = {}
        for i, (at_step, way, halves, owner, target, adds) in enumerate(sends):
            if at_step != step:
                continue
            if phase == 1:
                values = product(g, halves[0], owner)
            else:
                packed = packed_rows(g)
                n = sum(packed)
                values = []
                for h in halves:
                    first = pl.multiple_of(at(ring, owner) * n, n) + (packed[0] if h else 0)
                    values.append(buf[g, "pack"][pl.ds(pl.multiple_of(first, 16), packed[h]), :])
            own[i] = values
        for i, values in own.items():
            _, _, halves, _, target, adds = sends[i]
            blocks = blocks_of(g, phase, halves)
            for j in adds:
                copies[g, phase, j].wait_recv()
                came = received(g, phase, j)
                values = [v + came[key] if key in came else v for v, (key, _) in zip(values, blocks)]
            row, n = spot[g, phase, i]
            src, dst = (buf[g, f"{side}{phase}"].at[pl.ds(row, n), :] for side in "sr")
            for value, (_, rows_now) in zip(values, blocks):
                buf[g, f"s{phase}"][row : row + rows_now, :] = value.astype(BF16)
                row += rows_now
            number = numbers[g, phase, i]
            copies[g, phase, i] = remote(src, dst, ssem.at[number], rsem.at[number], neighbour(ring, target))

    def arrived(g, phase, h, values):
        for i, (_, _, halves, owner, target, _) in enumerate(routes[g, phase][1]):
            if owner == target and h in halves:
                if (g, phase, i) not in waited:
                    waited.add((g, phase, i))
                    copies[g, phase, i].wait_recv()
                came = received(g, phase, i)
                values = [v + came[key] for v, (key, _) in zip(values, blocks_of(g, phase, (h,)))]
        return values

    waited = set()

    def close_first(g):
        axis, halves, _ = GROUPS[g]
        packed = packed_rows(g)
        first = 0
        for h, half in enumerate(halves):
            full_sum, pack = buf[g, h, "sum"], buf[g, "pack"]
            for t, tile in enumerate(arrived(g, 1, h, product(g, h, 0))):
                if tile.shape[0] < full_sum.shape[0]:
                    tile = unfold(tile)
                full_sum[:, LANE * t : LANE * t + LANE] = tile
            for o in range(NZ if axis == "x" else NX):
                for t in range(width_of(half) // LANE):
                    to = o * sum(packed) + OWN * (first + t)
                    pack[to : to + OWN, :] = full_sum[OWN * o : OWN * o + OWN, LANE * t : LANE * t + LANE]
            first += width_of(half) // LANE

    out = {"gate": gate_ref, "up": up_ref, "down": down_ref}

    def close_second(g):
        axis, halves, _ = GROUPS[g]
        packed = packed_rows(g)
        n = sum(packed)
        pack = buf[g, "pack"]
        base = mine["z" if axis == "x" else "x"] * n
        for h in range(2):
            row = packed[0] if h else 0
            own = pack[pl.ds(pl.multiple_of(pl.multiple_of(base, n) + row, 16), packed[h]), :]
            (fin[row : row + packed[h], :],) = arrived(g, 2, h, [own])
        row = 0
        for src, lo, hi in halves[0] + halves[1]:
            for start in range(lo, hi, LANE):
                width = min(LANE, hidden - start)
                out[src][:, start : start + width] = fin[row : row + OWN, 0:width]
                row += OWN

    for g, phase, step in ORDER:
        if phase == 0:
            close_first(g)
        elif phase == 3:
            close_second(g)
        else:
            send(g, phase, step)

    for copy in sent:
        copy.wait_send()


def add_noise(gate_ref, up_ref, down_ref, ng_ref, nu_ref, nd_ref, gate_out, up_out, down_out):
    gate_out[...] = gate_ref[...] + ng_ref[...]
    up_out[...] = up_ref[...] + nu_ref[...]
    down_out[...] = down_ref[...] + nd_ref[...]


def per_device(
    n_f, inputs, cotangent, gate_weight, up_weight, down_weight, live_counts, noise_gate, noise_up, noise_down
):
    rows = inputs.shape[0]
    seq = rows // SLOTS
    hidden = gate_weight.shape[1]
    full = hidden // 256 * 256
    bound = 0.1 * math.sqrt(SEQ * D * FF)
    any_spec = pl.BlockSpec(memory_space=pl.ANY)
    vmem = pl.BlockSpec(memory_space=pltpu.VMEM)
    dma = pltpu.SemaphoreType.DMA
    out = jax.ShapeDtypeStruct((OWN, hidden), F32)
    held = pltpu.VMEM((OWN, hidden), F32)
    gate, up, down = pl.pallas_call(
        functools.partial(kernel, n_f, seq, hidden, bound),
        out_shape=(held, held, held),
        in_specs=[pl.BlockSpec(memory_space=pltpu.SMEM)] + [any_spec] * 5,
        out_specs=(vmem, vmem, vmem),
        scratch_shapes=[
            pltpu.VMEM((rows, D), BF16),
            pltpu.VMEM((rows, D), BF16),
            pltpu.VMEM((full, D), BF16),
            pltpu.VMEM((full, D), BF16),
            pltpu.VMEM((2 * LANE, D), BF16),
            pltpu.VMEM((hidden, D), BF16),
            pltpu.VMEM((rows, HP), BF16),
            pltpu.VMEM((rows, HP), BF16),
            pltpu.VMEM((rows, HP), BF16),
            pltpu.VMEM((SLOTS, seq, seq), F32),
            pltpu.VMEM((D, rows), F32),
            pltpu.VMEM((D, rows), F32),
            pltpu.VMEM((D, rows), BF16),
            pltpu.VMEM((D, rows), BF16),
            pltpu.VMEM((D, rows), BF16),
            pltpu.VMEM((8, LANE), F32),
            pltpu.VMEM((max(n_f - 1, 1), 8, LANE), F32),
            pltpu.VMEM((max(sum(packed_rows(g)) for g in range(len(GROUPS))), LANE), F32),
            dma((2 + 3 * (full // 256) + 3,)),
            dma((max(n_f - 1, 1),)),
            dma((max(n_f - 1, 1),)),
            dma((total_sends(),)),
            dma((total_sends(),)),
        ]
        + [pltpu.VMEM(shape, dtype) for shape, dtype in scratch_plan().values()],
        compiler_params=pltpu.CompilerParams(
            collective_id=0, has_side_effects=True, vmem_limit_bytes=60 * 1024 * 1024
        ),
    )(live_counts, inputs, cotangent, gate_weight.T, up_weight.T, down_weight)
    gate, up, down = pl.pallas_call(
        add_noise,
        out_shape=(out, out, out),
        in_specs=[vmem] * 6,
        out_specs=(vmem, vmem, vmem),
        compiler_params=pltpu.CompilerParams(vmem_limit_bytes=4 * 1024 * 1024),
    )(gate, up, down, noise_gate, noise_up, noise_down.T)
    return gate, up, down.T


def solution(mesh):
    in_specs = (
        P("dp", None),
        P("dp", None),
        P(None, "fsdp"),
        P(None, "fsdp"),
        P("fsdp", None),
        P("dp"),
        P("dp", "fsdp"),
        P("dp", "fsdp"),
        P("fsdp", "dp"),
    )
    out_specs = (P("dp", "fsdp"), P("dp", "fsdp"), P("fsdp", "dp"))
    return jax.shard_map(
        functools.partial(per_device, mesh.shape["fsdp"]),
        mesh=mesh, in_specs=in_specs, out_specs=out_specs, check_vma=False,
    )
```
